256 devices in a mesh: branch: 4 (over y), leaf: 64 (over x, z, core).
Axes of the slice: x: 4, y: 4, z: 8, core: 2. Of those that a mesh axis runs over, the one named last changes fastest.
Arguments:
- charges: bfloat16 [262144, 128], P(('branch', 'leaf')), may hold values from -6 to 6
- near_src: int32 [4096, 12], P(('branch', 'leaf')), may hold values from 0 to 4095, as said below
- near_block: bfloat16 [4096, 64, 768], P(('branch', 'leaf')), may hold values from -0.21875 to 0.21875
- bases: bfloat16 [4096, 64, 128], P(('branch', 'leaf')), may hold values from -0.75 to 0.75
- transfers: bfloat16 [4096, 64, 128], P(('branch', 'leaf')), may hold values from -0.1875 to 0.1875
- couple: bfloat16 [4096, 64, 192], P(('branch', 'leaf')), may hold values from -0.75 to 0.75
- far_dev: int32 [4096, 3], P(('branch', 'leaf')), may hold values from 0 to 63, all different within a row; in each aligned block of 16 rows (0 to 15, 16 to 31, ...) at most 2 rows name the same one
- far_leaf: int32 [4096, 3], P(('branch', 'leaf')), may hold values from 0 to 15
- upper_couple: bfloat16 [256, 64, 128], P(('branch', 'leaf')), may hold values from -0.5 to 0.5
- upper_src: int32 [256, 2], P(('branch', 'leaf')), may hold values from 1 to 3
Outputs:
- potentials: bfloat16 [262144, 128], P(('branch', 'leaf'))
The draws below stay inside these ranges and needn't reach their ends.
Inputs may be any that keep to these rules, and one draw needn't show every extreme that they name: near_src[s,k] lies in the same group of 1024 consecutive leaves as s and at most 8 leaves from s; that distance is reached. `far_dev`: within the rows of one device (aligned blocks of 16 rows), no value occurs more than 2 times, and some value occurs exactly 2 times.
All inputs are finite; a program needn't handle non-finite values.
Results may differ from the reference program's by a relative error of at most 0.0059.
Values may be sent and summed in bfloat16 or wider, within the bound.
A program may use at most 64 MiB of HBM per device.

```python
import math
import jax
import jax.numpy as jnp
import numpy as np
from jax import lax

LEAF = 64
RANK = 64
NRHS = 128
LEAF_DEV = 16
NEAR = 12
FAR = 3
HALO = 8
KU = 2
CAP = 2
BRANCH_LEAVES = 1024
LEAVES = 4096
PARENTS = 256
POINTS = 262144
N_BRANCH = 4
N_LEAF = 64


def draw_near_src(key, part):
    key = jax.random.fold_in(key, 11)
    offsets = jax.random.randint(key, (LEAVES, NEAR), -HALO, HALO + 1, dtype=jnp.int32)
    column = jnp.arange(NEAR, dtype=jnp.int32)[None, :]
    offsets = jnp.where(column == 0, -HALO, jnp.where(column == 1, HALO, offsets))
    leaves = jnp.arange(LEAVES, dtype=jnp.int32)[:, None]
    lowest = leaves // BRANCH_LEAVES * BRANCH_LEAVES
    return jnp.clip(leaves + offsets, lowest, lowest + BRANCH_LEAVES - 1).astype(jnp.int32)


def place_ends(drawn, rng, least, top_value):
    place = [jax.random.randint(jax.random.fold_in(rng, axis), (), 0, length) for axis, length in enumerate(drawn.shape)]
    widest = drawn.shape.index(max(drawn.shape))
    next_to = place[:widest] + [(place[widest] + 1) % drawn.shape[widest]] + place[widest + 1:]
    return drawn.at[tuple(place)].set(least).at[tuple(next_to)].set(top_value)


def steps_of(key, extent, cuts, least, largest):
    gain, own = 1.0, jax.random.fold_in(key, 6)
    for axis_at, parts in cuts:
        draws = jnp.exp(jax.random.uniform(jax.random.fold_in(own, axis_at), (parts,), jnp.float32, least / len(cuts), largest / len(cuts)))
        gain = gain * jnp.repeat(draws, extent[axis_at] // parts).reshape([-1 if axis == axis_at else 1 for axis in range(len(extent))])
    return gain


def deal_out(own_key, own, number, rows, number_of, top, reach, lean):
    order = jax.random.permutation(own_key, number_of)
    crowded, common = shares(number_of, rows * top, reach, lean, True), shares(number_of, rows * top, reach, lean, False)
    places = jnp.arange(number_of)

    def named(lengths, offset_by):
        used = int((lengths > 0).sum())
        fixed = max(1, used // 4)
        moved = fixed + (places - fixed + offset_by * (used - fixed)) % max(1, number_of - fixed)
        return jnp.zeros((number_of,), jnp.int32).at[order[jnp.where(places < fixed, places, moved)]].set(jnp.asarray(lengths, jnp.int32))

    lengths = jnp.where(number % 4 == 0, named(crowded, number // 4), named(common, number - number // 4 - 1))
    mixed = jax.random.permutation(jax.random.fold_in(own, 3), number_of)
    donor, receiver = mixed[0:number_of // 2 * 2:2], mixed[1:number_of // 2 * 2:2]
    room = jnp.minimum(lengths[donor] - 1, reach - lengths[receiver]) // 2
    room = jnp.where((donor == order[0]) | (receiver == order[0]) | (lengths[receiver] == 0), 0, jnp.maximum(room, 0))
    moved = jax.random.randint(jax.random.fold_in(own, 4), (number_of // 2,), 0, 1 << 20) % (room + 1)
    lengths = lengths.at[donor].add(-moved).at[receiver].add(moved)
    items = jnp.searchsorted(jnp.cumsum(lengths), jnp.arange(rows * top), side="right").astype(jnp.int32)
    table = items.reshape(top, rows).T
    table = table[jax.random.permutation(jax.random.fold_in(own, 1), rows)]
    offset_by = jax.random.randint(jax.random.fold_in(own, 2), (rows, 1), 0, top)
    return jnp.take_along_axis(table, (jnp.arange(top)[None, :] + offset_by) % top, axis=1)


def shares(count, total, reach, skew, full):
    portions = [(1 << 20) // math.isqrt(standing ** skew) + 1 for standing in range(1, count + 1)]
    largest = reach if full else min(reach, max(-(-total // count), total * portions[0] // sum(portions)))
    least = 1 if total - largest >= count - 1 else 0
    given, rest = [largest] + [least] * (count - 1), total - largest - least * (count - 1)
    while rest > 0:
        movable = [i for i in range(1, count) if given[i] < largest] or [i for i in range(1, count) if given[i] < reach]
        pool, left = sum([portions[i] for i in movable]), rest
        for i in movable:
            more = min(reach - given[i], max(1, left * portions[i] // pool), rest)
            given[i] = given[i] + more
            rest = rest - more
    return np.array(given)


def scatter_about(key, shape, scale, most, pieces=(), kind=jnp.bfloat16):
    level = steps_of(key, shape, pieces, -0.22, 0.18) if pieces else 1.0
    entries = jax.random.normal(key, shape, jnp.float32) * scale * level
    return jnp.minimum(jnp.maximum(entries, -most), most).astype(kind)


def setup_inputs(seed: int = 0) -> dict:
    arg_keys = jax.random.split(jax.random.key(seed), 11)
    charges = scatter_about(arg_keys[0], (POINTS, NRHS), 1.0, 6.0, ((0, 256),))
    near_src = draw_near_src(jax.random.fold_in(arg_keys[10], 71), 0)
    near_block = scatter_about(arg_keys[2], (LEAVES, LEAF, NEAR * LEAF), (LEAF * NEAR) ** -0.5, 0.21875, ((0, 256),))
    bases = scatter_about(arg_keys[3], (LEAVES, LEAF, 2 * RANK), LEAF ** -0.5, 0.75, ((0, 256),))
    transfers = scatter_about(arg_keys[4], (LEAVES, RANK, 2 * RANK), (RANK * LEAF_DEV) ** -0.5, 0.1875, ((0, 256),))
    couple = scatter_about(arg_keys[5], (LEAVES, RANK, FAR * RANK), RANK ** -0.5, 0.75, ((0, 256),))
    far_dev_keys = jax.random.split(jax.random.fold_in(arg_keys[6], 1), LEAVES // LEAF_DEV)
    far_dev_turns = jax.random.permutation(jax.random.fold_in(arg_keys[6], 3), LEAVES // LEAF_DEV)
    far_dev = jax.vmap(lambda own, number: deal_out(jax.random.fold_in(arg_keys[6], 2), own, number, LEAF_DEV, N_LEAF, FAR, CAP, 2))(far_dev_keys, far_dev_turns).reshape((LEAVES, FAR))
    far_leaf = place_ends(jax.random.randint(arg_keys[7], (LEAVES, FAR), 0, LEAF_DEV), jax.random.fold_in(arg_keys[7], 1), 0, LEAF_DEV - 1).astype(jnp.int32)
    upper_couple = scatter_about(arg_keys[8], (PARENTS, RANK, KU * RANK), (RANK * KU) ** -0.5, 0.5, ((0, 256),))
    upper_src = place_ends(jax.random.randint(arg_keys[9], (PARENTS, KU), 1, N_BRANCH), jax.random.fold_in(arg_keys[9], 1), 1, N_BRANCH - 1).astype(jnp.int32)
    return dict(charges=charges, near_src=near_src, near_block=near_block, bases=bases, transfers=transfers, couple=couple, far_dev=far_dev, far_leaf=far_leaf, upper_couple=upper_couple, upper_src=upper_src)


def settle(value):
    return lax.optimization_barrier(value.astype(jnp.bfloat16)).astype(jnp.float32)


def reference(charges, near_src, near_block, bases, transfers, couple, far_dev, far_leaf, upper_couple, upper_src):
    blocks = LEAVES // LEAF_DEV
    points = charges.reshape(LEAVES, LEAF, NRHS).astype(jnp.float32)
    row_basis = bases[:, :, :RANK].astype(jnp.float32)
    col_basis = bases[:, :, RANK:].astype(jnp.float32)
    coeff = settle(jnp.einsum('lpr,lpn->lrn', row_basis, points))
    row_transfer = transfers[:, :, :RANK].astype(jnp.float32).reshape(PARENTS, LEAF_DEV, RANK, RANK)
    col_transfer = transfers[:, :, RANK:].astype(jnp.float32).reshape(PARENTS, LEAF_DEV, RANK, RANK)
    parent_coeff = settle(jnp.einsum('plrq,plrn->pqn', row_transfer, coeff.reshape(PARENTS, LEAF_DEV, RANK, NRHS)))
    parent_ids = jnp.arange(PARENTS, dtype=jnp.int32)
    own_group = (parent_ids // N_LEAF)[:, None]
    sources = ((own_group + upper_src) % N_BRANCH) * N_LEAF + (parent_ids % N_LEAF)[:, None]
    upper_blocks = upper_couple.astype(jnp.float32).reshape(PARENTS, RANK, KU, RANK)
    parent_down = settle(jnp.einsum('prkq,pkrn->pqn', upper_blocks, parent_coeff[sources]))
    group_start = (jnp.arange(LEAVES, dtype=jnp.int32) // BRANCH_LEAVES) * BRANCH_LEAVES
    targets = group_start[:, None] + far_dev * LEAF_DEV + far_leaf

    def far_step(total, index):
        start = index * LEAF_DEV
        blocks_here = lax.dynamic_slice_in_dim(couple, start, LEAF_DEV, 0).astype(jnp.float32).reshape(LEAF_DEV, RANK, FAR, RANK)
        coeff_here = lax.dynamic_slice_in_dim(coeff, start, LEAF_DEV, 0)
        target_here = lax.dynamic_slice_in_dim(targets, start, LEAF_DEV, 0)
        coupled = settle(jnp.einsum('lrkq,lrn->lkqn', blocks_here, coeff_here))
        total = total.at[target_here.reshape(-1)].add(coupled.reshape(LEAF_DEV * FAR, RANK, NRHS))
        return total, None

    far_total, unused = lax.scan(far_step, jnp.zeros((LEAVES, RANK, NRHS), jnp.float32), jnp.arange(blocks, dtype=jnp.int32))
    from_parent = jnp.einsum('plrq,pqn->plrn', col_transfer, parent_down).reshape(LEAVES, RANK, NRHS)
    down = settle(far_total + from_parent)
    far_out = jnp.einsum('lpr,lrn->lpn', col_basis, down)

    def near_step(index):
        start = index * LEAF_DEV
        block_here = lax.dynamic_slice_in_dim(near_block, start, LEAF_DEV, 0).astype(jnp.float32).reshape(LEAF_DEV, LEAF, NEAR, LEAF)
        source_here = lax.dynamic_slice_in_dim(near_src, start, LEAF_DEV, 0)
        gathered = points[source_here]
        return jnp.einsum('lpks,lkpn->lsn', block_here, gathered)

    near_out = lax.map(near_step, jnp.arange(blocks, dtype=jnp.int32)).reshape(LEAVES, LEAF, NRHS)
    return (far_out + near_out).astype(jnp.bfloat16).reshape(POINTS, NRHS)
```

```python
import jax
import jax.numpy as jnp
from jax import lax
from jax.experimental import pallas as pl
from jax.experimental.pallas import tpu as pltpu
from jax.sharding import PartitionSpec as P

LEAF = 64
RANK = 64
NRHS = 128
LEAF_DEV = 16
NEAR = 12
FAR = 3
HALO = 8
KU = 2
PAIRS = LEAF_DEV * FAR
EMPTY = PAIRS * 32 + LEAF_DEV
MESH = pl.DeviceIdType.MESH
BF = jnp.bfloat16
F32 = jnp.float32


def tdot(a, b):
    return lax.dot_general(a, b, (((0,), (0,)), ((), ())), preferred_element_type=F32)


def dot(a, b):
    return jnp.dot(a, b, preferred_element_type=F32)


def step_of(i):
    far = 4 - (i + 1) // 2
    return far if i % 2 == 1 or i == 0 else -far


def kernel(
    fd, fl, ns, us, charges, near_block, bases, transfers, couple, upper,
    out,
    pad, nb, bv, tv, cv, uv, coeff, cpl, idxv, idxs, lab, labr, xs, xr, vrow, zs, zr, pcs, pcr,
    down_from_parent, near, downs,
    load_sem, idx_sem, halo_ss, halo_rs, lab_ss, lab_rs, pc_ss, pc_rs, xs_sem, xr_sem, zs_sem, zr_sem,
):
    b = lax.axis_index("branch")
    me = lax.axis_index("leaf")
    c = me % 2
    z = (me // 2) % 8
    x = me // 16
    g = x * 2 + c
    left = (b, (me + 63) % 64)
    right = (b, (me + 1) % 64)
    up = (b, (x * 8 + (z + 1) % 8) * 2 + c)
    low = (b, (x * 8 + (z + 7) % 8) * 2 + c)

    def member(k):
        other = (g + k) % 8
        return other, (b, ((other // 2) * 8 + z) * 2 + other % 2)

    def group(k):
        return ((b + k) % 4, me)

    mine = pad.at[pl.ds(HALO, LEAF_DEV)]
    loads = [
        pltpu.make_async_copy(src, dst, load_sem.at[n])
        for n, (src, dst) in enumerate(
            [(charges, mine), (bases, bv), (couple, cv), (transfers, tv), (upper, uv), (near_block, nb)]
        )
    ]
    for load in loads:
        load.start()

    barrier = pltpu.get_barrier_semaphore()
    partners = [member(k)[1] for k in range(1, 8)] + [up, low, left, right] + [group(k) for k in range(1, 4)]
    for partner in partners:
        pl.semaphore_signal(barrier, inc=1, device_id=partner, device_id_type=MESH)

    lane = lax.broadcasted_iota(jnp.int32, (8, 128), 1)
    row = lax.broadcasted_iota(jnp.int32, (8, 128), 0)
    one = jnp.full((8, 128), EMPTY, jnp.int32)
    two = jnp.full((8, 128), EMPTY, jnp.int32)
    for t in range(LEAF_DEV):
        for k in range(FAR):
            code = (t * FAR + k) * 32 + fl[t, k]
            hit = lane == fd[t, k]
            taken = one != EMPTY
            two = jnp.where(hit & taken, code, two)
            one = jnp.where(hit & ~taken, code, one)
    code = jnp.where(row == 0, one, jnp.where(row == 1, two, EMPTY))
    idxv[...] = code >> 5
    to_scalars = pltpu.make_async_copy(idxv, idxs, idx_sem)
    to_scalars.start()
    lab[...] = (code & 31).astype(F32)

    loads[0].wait()
    loads[1].wait()

    def coeff_step(t, carry):
        coeff[t] = tdot(bv[t], pad[t + HALO])[:RANK].astype(BF)
        return carry

    lax.fori_loop(0, LEAF_DEV, coeff_step, 0, unroll=True)

    pl.semaphore_wait(barrier, len(partners))

    def halo_copy(n):
        src = pad.at[pl.ds(LEAF_DEV if n == 0 else HALO, HALO)]
        dst = pad.at[pl.ds(0 if n == 0 else HALO + LEAF_DEV, HALO)]
        return pltpu.make_async_remote_copy(
            src, dst, halo_ss.at[n], halo_rs.at[n], device_id=(right, left)[n], device_id_type=MESH
        )

    for n in range(2):
        halo_copy(n).start()

    def lab_copy(k):
        return pltpu.make_async_remote_copy(
            lab, labr.at[g], lab_ss, lab_rs, device_id=member(k)[1], device_id_type=MESH
        )

    def lab_step(k, carry):
        lab_copy(k).start()
        return carry

    lax.fori_loop(1, 8, lab_step, 0)
    labr[g] = lab[...]

    loads[2].wait()

    def couple_step(t, carry):
        product = tdot(cv[t], coeff[t]).astype(BF)
        cpl[pl.ds(t * FAR, FAR)] = product.reshape(FAR, 4, 16, NRHS)
        return carry

    lax.fori_loop(0, LEAF_DEV, couple_step, 0, unroll=True)
    cpl[PAIRS] = jnp.zeros((4, 16, NRHS), BF)
    to_scalars.wait()

    def z_of(i):
        return (z + step_of(i) + 8) % 8

    def fill(i):
        def fill_step(other, carry):
            device = ((other // 2) * 8 + z_of(i)) * 2 + other % 2
            for slot in range(2):
                xs[other, i, :, slot * 16:(slot + 1) * 16, :] = cpl[idxs[slot, device]]
            return carry

        lax.fori_loop(0, 8, fill_step, 0, unroll=True)
        xr[i, :, g] = xs[g, i]

    def send_x(i, h):
        def send_step(k, carry):
            other, target = member(k)
            pltpu.make_async_remote_copy(
                xs.at[other, i, pl.ds(2 * h, 2)],
                xr.at[i, pl.ds(2 * h, 2), g],
                xs_sem,
                xr_sem.at[i, h],
                device_id=target,
                device_id_type=MESH,
            ).start()
            return carry

        lax.fori_loop(1, 8, send_step, 0, unroll=True)

    rounds = [(0,), (1, 2), (3, 4), (5, 6), (7,)]
    for chunks in rounds:
        for i in chunks:
            fill(i)
        for h in range(2):
            for i in chunks:
                send_x(i, h)

    loads[3].wait()
    packed = tdot(tv[...].reshape(LEAF_DEV * RANK, 2 * RANK), coeff[...].reshape(LEAF_DEV * RANK, NRHS))
    pcs[...] = packed[:RANK].astype(BF)

    def pc_copy(k):
        return pltpu.make_async_remote_copy(
            pcs, pcr.at[3 - k], pc_ss.at[k - 1], pc_rs.at[3 - k], device_id=group(k), device_id_type=MESH
        )

    for k in range(1, 4):
        pc_copy(k).start()

    pltpu.make_async_copy(labr.at[pl.ds(0, 7)], labr.at[pl.ds(0, 7)], lab_rs).wait()
    spread_row = lax.broadcasted_iota(jnp.int32, (64, 256), 0)
    spread_col = lax.broadcasted_iota(jnp.int32, (64, 256), 1)
    spread = (spread_row // 8 == spread_col // 32) & (spread_row % 8 == (spread_col // 16) % 2)
    by_device = tdot(labr[...].reshape(64, 128).astype(BF), spread.astype(F32).astype(BF)).astype(BF)
    chunk = lax.broadcasted_iota(jnp.int32, (16, 128), 0)
    far = 4 - (chunk + 1) // 2
    chunk_z = (z + jnp.where(chunk % 2 == 1, far, -far) + 16) % 8
    pick = lax.broadcasted_iota(jnp.int32, (16, 128), 1) == (x * 8 + chunk_z) * 2 + c
    labels = dot(pick.astype(F32).astype(BF), by_device)
    column = lax.broadcasted_iota(jnp.int32, (16, 256), 1)
    vrow[...] = labels * 16.0 + (column % 16).astype(F32)

    first = (b * 64 + me) * LEAF_DEV - HALO

    def near_step(s, carry):
        tall = jnp.concatenate([nb[s, :, 128 * j:128 * (j + 1)] for j in range(NEAR // 2)], axis=0)
        even = jnp.concatenate([pad[(ns[s, 2 * j] - first) & 31] for j in range(NEAR // 2)], axis=0)
        odd = jnp.concatenate([pad[(ns[s, 2 * j + 1] - first) & 31] for j in range(NEAR // 2)], axis=0)
        both = tdot(tall, jnp.concatenate([even, odd], axis=1))
        near[s] = both[:LEAF, :NRHS] + both[LEAF:, NRHS:]
        return carry

    def parents():
        loads[4].wait()
        for k in range(1, 4):
            pc_copy(k).wait_recv()
        picked = jnp.concatenate([pcr[jnp.clip(us[0, k] - 1, 0, 2)] for k in range(KU)], axis=1)
        both = tdot(uv[0], picked)
        parent_down = (both[:RANK, :NRHS] + both[RANK:, NRHS:]).astype(BF)
        lifted = jnp.concatenate([jnp.zeros((RANK, NRHS), BF), parent_down], axis=0)
        down_from_parent[...] = dot(tv[...].reshape(LEAF_DEV * RANK, 2 * RANK), lifted).reshape(
            LEAF_DEV, 4, 16, NRHS
        )

    tall_row = lax.broadcasted_iota(jnp.int32, (256, 256), 0).astype(F32)

    def slots(i, h):
        region = xr.at[i, pl.ds(2 * h, 2), pl.ds(0, 7)]
        pltpu.make_async_copy(region, region, xr_sem.at[i, h]).wait()
        hot = jnp.where(tall_row == vrow[i:i + 1, :], 1.0, 0.0).astype(BF)
        blocks = jnp.concatenate([xr[i, 2 * h + q].reshape(256, NRHS) for q in range(2)], axis=1)
        sums = dot(hot, blocks)
        return [sums[:, q * NRHS:(q + 1) * NRHS] for q in range(2)]

    def z_copy(i, h, sign):
        rows = pl.ds(0, 256) if i else pl.ds(0 if sign > 0 else 128, 128)
        place = 7 if i == 0 and sign < 0 else i
        return pltpu.make_async_remote_copy(
            zs.at[i, h, :, rows],
            zr.at[i, h, :, rows],
            zs_sem.at[place, h],
            zr_sem.at[place, h],
            device_id=up if sign > 0 else low,
            device_id_type=MESH,
        )

    def unit(i, h):
        sums = slots(i, h)
        if i == 0:
            for q in range(2):
                zs[i, h, q] = sums[q].astype(BF)
            z_copy(i, h, 1).start()
            z_copy(i, h, -1).start()
            return
        if i == 7:
            z_copy(5, h, 1).wait_recv()
            z_copy(6, h, -1).wait_recv()
            for q in range(2):
                total = sums[q] + zr[5, h, q].astype(F32) + zr[6, h, q].astype(F32)
                total = total.reshape(LEAF_DEV, 16, NRHS) + down_from_parent[:, 2 * h + q]
                downs[:, 2 * h + q] = total.astype(BF)
            return
        sign = 1 if i % 2 else -1
        before = max(i - 2, 0)
        z_copy(before, h, sign).wait_recv()
        for q in range(2):
            if before:
                zs[i, h, q] = (sums[q] + zr[before, h, q].astype(F32)).astype(BF)
            else:
                met = slice(0, 128) if sign > 0 else slice(128, 256)
                rest = slice(128, 256) if sign > 0 else slice(0, 128)
                zs[i, h, q, met] = (sums[q][met] + zr[0, h, q, met].astype(F32)).astype(BF)
                zs[i, h, q, rest] = sums[q][rest].astype(BF)
        z_copy(i, h, sign).start()

    unit(0, 0)
    unit(0, 1)
    for n in range(2):
        halo_copy(n).wait_recv()
    loads[5].wait()
    done = 0
    for chunks in rounds[1:4]:
        for h in range(2):
            for i in chunks:
                unit(i, h)
                if done == 0:
                    parents()
                if done < 8:
                    lax.fori_loop(2 * done, 2 * done + 2, near_step, 0, unroll=True)
                done += 1

    sent = xs.at[pl.ds(0, 7)]
    unit(7, 0)
    unit(7, 1)

    def out_step(s, carry):
        down = downs[s].reshape(RANK, NRHS)
        lifted = jnp.concatenate([jnp.zeros((RANK, NRHS), BF), down], axis=0)
        out[s] = (dot(bv[s], lifted) + near[s]).astype(BF)
        return carry

    lax.fori_loop(0, LEAF_DEV, out_step, 0, unroll=True)

    pltpu.make_async_copy(sent, sent, xs_sem).wait()
    for n in range(2):
        halo_copy(n).wait_send()
    pltpu.make_async_copy(labr.at[pl.ds(0, 7)], labr.at[pl.ds(0, 7)], lab_ss).wait()
    for k in range(1, 4):
        pc_copy(k).wait_send()
    for h in range(2):
        z_copy(0, h, -1).wait_send()
        for i in range(7):
            z_copy(i, h, 1 if i == 0 or i % 2 else -1).wait_send()


def per_device(
    charges, near_src, near_block, bases, transfers, couple, far_dev, far_leaf, upper_couple, upper_src
):
    smem = pl.BlockSpec(memory_space=pltpu.SMEM)
    hbm = pl.BlockSpec(memory_space=pl.ANY)
    dma = pltpu.SemaphoreType.DMA
    out = pl.pallas_call(
        kernel,
        name="adjoint",
        out_shape=jax.ShapeDtypeStruct((LEAF_DEV, LEAF, NRHS), BF),
        in_specs=[smem] * 4 + [hbm] * 6,
        out_specs=pl.BlockSpec(memory_space=pltpu.VMEM),
        scratch_shapes=[
            pltpu.VMEM((LEAF_DEV + 2 * HALO, LEAF, NRHS), BF),
            pltpu.VMEM((LEAF_DEV, LEAF, NEAR * LEAF), BF),
            pltpu.VMEM((LEAF_DEV, LEAF, 2 * RANK), BF),
            pltpu.VMEM((LEAF_DEV, RANK, 2 * RANK), BF),
            pltpu.VMEM((LEAF_DEV, RANK, FAR * RANK), BF),
            pltpu.VMEM((1, RANK, KU * RANK), BF),
            pltpu.VMEM((LEAF_DEV, RANK, NRHS), BF),
            pltpu.VMEM((PAIRS + 1, 4, 16, NRHS), BF),
            pltpu.VMEM((8, 128), jnp.int32),
            pltpu.SMEM((8, 128), jnp.int32),
            pltpu.VMEM((8, 128), F32),
            pltpu.VMEM((8, 8, 128), F32),
            pltpu.VMEM((8, 8, 4, 32, NRHS), BF),
            pltpu.VMEM((8, 4, 8, 32, NRHS), BF),
            pltpu.VMEM((16, 256), F32),
            pltpu.VMEM((7, 2, 2, 256, NRHS), BF),
            pltpu.VMEM((7, 2, 2, 256, NRHS), BF),
            pltpu.VMEM((RANK, NRHS), BF),
            pltpu.VMEM((3, RANK, NRHS), BF),
            pltpu.VMEM((LEAF_DEV, 4, 16, NRHS), F32),
            pltpu.VMEM((LEAF_DEV, LEAF, NRHS), F32),
            pltpu.VMEM((LEAF_DEV, 4, 16, NRHS), BF),
            dma((6,)),
            dma,
            dma((2,)),
            dma((2,)),
            dma,
            dma,
            dma((3,)),
            dma((3,)),
            dma,
            dma((8, 2)),
            dma((8, 2)),
            dma((8, 2)),
        ],
        compiler_params=pltpu.CompilerParams(
            collective_id=0, has_side_effects=True, vmem_limit_bytes=56 * 1024 * 1024
        ),
    )(
        far_dev, far_leaf, near_src, upper_src,
        charges.reshape(LEAF_DEV, LEAF, NRHS), near_block, bases, transfers, couple, upper_couple,
    )
    return out.reshape(LEAF_DEV * LEAF, NRHS)


def solution(mesh):
    rows = P(("branch", "leaf"), None)
    blocks = P(("branch", "leaf"), None, None)
    in_specs = (rows, rows, blocks, blocks, blocks, blocks, rows, rows, blocks, rows)
    return jax.shard_map(per_device, mesh=mesh, in_specs=in_specs, out_specs=rows, check_vma=False)
```

```python
import jax
import jax.numpy as jnp
from jax import lax
from jax.experimental import pallas as pl
from jax.experimental.pallas import tpu as pltpu
from jax.sharding import PartitionSpec as P

LEAF = 64
RANK = 64
NRHS = 128
LEAF_DEV = 16
NEAR = 12
FAR = 3
HALO = 8
KU = 2
PAIRS = LEAF_DEV * FAR
EMPTY = PAIRS * 32 + LEAF_DEV
MESH = pl.DeviceIdType.MESH
BF = jnp.bfloat16
F32 = jnp.float32


def tdot(a, b):
    return lax.dot_general(a, b, (((0,), (0,)), ((), ())), preferred_element_type=F32)


def dot(a, b):
    return jnp.dot(a, b, preferred_element_type=F32)


def step_of(i):
    far = 4 - (i + 1) // 2
    return far if i % 2 == 1 or i == 0 else -far


def kernel(
    fd_hbm, fl_hbm, ns_hbm, us_hbm, charges, near_block, bases, transfers, couple, upper,
    out,
    fd, fl, ns, us, pad, nb, bv, tv, cv, uv, coeff, cpl, idxv, idxs, lab, labr, xs, xr, vrow, zs, zr, pcs, pcr,
    down_from_parent, near, downs,
    load_sem, idx_sem, halo_ss, halo_rs, lab_ss, lab_rs, pc_ss, pc_rs, xs_sem, xr_sem, zs_sem, zr_sem,
):
    b = lax.axis_index("branch")
    me = lax.axis_index("leaf")
    c = me % 2
    z = (me // 2) % 8
    x = me // 16
    g = x * 2 + c
    left = (b, (me + 63) % 64)
    right = (b, (me + 1) % 64)
    up = (b, (x * 8 + (z + 1) % 8) * 2 + c)
    low = (b, (x * 8 + (z + 7) % 8) * 2 + c)

    def member(k):
        other = (g + k) % 8
        return other, (b, ((other // 2) * 8 + z) * 2 + other % 2)

    def group(k):
        return ((b + k) % 4, me)

    barrier = pltpu.get_barrier_semaphore()
    partners = [member(k)[1] for k in range(1, 8)] + [up, low, left, right] + [group(k) for k in range(1, 4)]
    for partner in partners:
        pl.semaphore_signal(barrier, inc=1, device_id=partner, device_id_type=MESH)

    mine = pad.at[pl.ds(HALO, LEAF_DEV)]
    loads = [
        pltpu.make_async_copy(src, dst, load_sem.at[n])
        for n, (src, dst) in enumerate(
            [
                (charges, mine), (bases, bv), (couple, cv), (transfers, tv), (upper, uv), (near_block, nb),
                (fd_hbm, fd), (fl_hbm, fl), (ns_hbm, ns), (us_hbm, us),
            ]
        )
    ]
    for n in (6, 7, 0, 1, 2):
        loads[n].start()

    loads[6].wait()
    loads[7].wait()
    lane = lax.broadcasted_iota(jnp.int32, (8, 128), 1)
    row = lax.broadcasted_iota(jnp.int32, (8, 128), 0)
    one = jnp.full((8, 128), EMPTY, jnp.int32)
    two = jnp.full((8, 128), EMPTY, jnp.int32)
    for t in range(LEAF_DEV):
        for k in range(FAR):
            code = (t * FAR + k) * 32 + fl[k, t]
            hit = lane == fd[k, t]
            taken = one != EMPTY
            two = jnp.where(hit & taken, code, two)
            one = jnp.where(hit & ~taken, code, one)
    code = jnp.where(row == 0, one, jnp.where(row == 1, two, EMPTY))
    idxv[...] = code >> 5
    to_scalars = pltpu.make_async_copy(idxv, idxs, idx_sem)
    to_scalars.start()
    lab[...] = (code & 31).astype(F32)

    loads[0].wait()
    loads[1].wait()

    def coeff_step(t, carry):
        coeff[t] = tdot(bv[t], pad[t + HALO])[:RANK].astype(BF)
        return carry

    lax.fori_loop(0, LEAF_DEV, coeff_step, 0, unroll=True)

    pl.semaphore_wait(barrier, len(partners))

    def halo_copy(n):
        src = pad.at[pl.ds(LEAF_DEV if n == 0 else HALO, HALO)]
        dst = pad.at[pl.ds(0 if n == 0 else HALO + LEAF_DEV, HALO)]
        return pltpu.make_async_remote_copy(
            src, dst, halo_ss.at[n], halo_rs.at[n], device_id=(right, left)[n], device_id_type=MESH
        )

    for n in range(2):
        halo_copy(n).start()

    def lab_copy(k):
        return pltpu.make_async_remote_copy(
            lab, labr.at[g], lab_ss, lab_rs, device_id=member(k)[1], device_id_type=MESH
        )

    def lab_step(k, carry):
        lab_copy(k).start()
        return carry

    lax.fori_loop(1, 8, lab_step, 0)
    labr[g] = lab[...]

    loads[2].wait()

    def couple_step(t, carry):
        product = tdot(cv[t], coeff[t]).astype(BF)
        cpl[pl.ds(t * FAR, FAR)] = product.reshape(FAR, 4, 16, NRHS)
        return carry

    lax.fori_loop(0, LEAF_DEV, couple_step, 0, unroll=True)
    cpl[PAIRS] = jnp.zeros((4, 16, NRHS), BF)
    to_scalars.wait()

    def z_of(i):
        return (z + step_of(i) + 8) % 8

    def fill(i):
        def fill_step(other, carry):
            device = ((other // 2) * 8 + z_of(i)) * 2 + other % 2
            for slot in range(2):
                xs[other, i, :, slot * 16:(slot + 1) * 16, :] = cpl[idxs[slot, device]]
            return carry

        lax.fori_loop(0, 8, fill_step, 0, unroll=True)
        xr[i, :, g] = xs[g, i]

    def send_x(i, h):
        def send_step(k, carry):
            other, target = member(k)
            pltpu.make_async_remote_copy(
                xs.at[other, i, pl.ds(2 * h, 2)],
                xr.at[i, pl.ds(2 * h, 2), g],
                xs_sem,
                xr_sem.at[i, h],
                device_id=target,
                device_id_type=MESH,
            ).start()
            return carry

        lax.fori_loop(1, 8, send_step, 0, unroll=True)

    rounds = [(0,), (1, 2), (3, 4), (5, 6), (7,)]

    def issue(chunks):
        for i in chunks:
            fill(i)
        for h in range(2):
            for i in chunks:
                send_x(i, h)

    issue(rounds[0])
    issue(rounds[1])
    for n in (3, 4, 5, 8, 9):
        loads[n].start()

    loads[3].wait()
    packed = tdot(tv[...].reshape(LEAF_DEV * RANK, 2 * RANK), coeff[...].reshape(LEAF_DEV * RANK, NRHS))
    pcs[...] = packed[:RANK].astype(BF)

    def pc_copy(k):
        return pltpu.make_async_remote_copy(
            pcs, pcr.at[3 - k], pc_ss.at[k - 1], pc_rs.at[3 - k], device_id=group(k), device_id_type=MESH
        )

    for k in range(1, 4):
        pc_copy(k).start()

    pltpu.make_async_copy(labr.at[pl.ds(0, 7)], labr.at[pl.ds(0, 7)], lab_rs).wait()
    spread_row = lax.broadcasted_iota(jnp.int32, (64, 256), 0)
    spread_col = lax.broadcasted_iota(jnp.int32, (64, 256), 1)
    spread = (spread_row // 8 == spread_col // 32) & (spread_row % 8 == (spread_col // 16) % 2)
    by_device = tdot(labr[...].reshape(64, 128).astype(BF), spread.astype(F32).astype(BF)).astype(BF)
    chunk = lax.broadcasted_iota(jnp.int32, (16, 128), 0)
    far = 4 - (chunk + 1) // 2
    chunk_z = (z + jnp.where(chunk % 2 == 1, far, -far) + 16) % 8
    pick = lax.broadcasted_iota(jnp.int32, (16, 128), 1) == (x * 8 + chunk_z) * 2 + c
    labels = dot(pick.astype(F32).astype(BF), by_device)
    column = lax.broadcasted_iota(jnp.int32, (16, 256), 1)
    vrow[...] = labels * 16.0 + (column % 16).astype(F32)

    first = (b * 64 + me) * LEAF_DEV - HALO

    def near_step(s, carry):
        tall = jnp.concatenate([nb[s, :, 128 * j:128 * (j + 1)] for j in range(NEAR // 2)], axis=0)
        even = jnp.concatenate([pad[(ns[s, 2 * j] - first) & 31] for j in range(NEAR // 2)], axis=0)
        odd = jnp.concatenate([pad[(ns[s, 2 * j + 1] - first) & 31] for j in range(NEAR // 2)], axis=0)
        both = tdot(tall, jnp.concatenate([even, odd], axis=1))
        near[s] = both[:LEAF, :NRHS] + both[LEAF:, NRHS:]
        return carry

    def parents():
        loads[4].wait()
        loads[9].wait()
        for k in range(1, 4):
            pc_copy(k).wait_recv()
        picked = jnp.concatenate([pcr[jnp.clip(us[0, k] - 1, 0, 2)] for k in range(KU)], axis=1)
        both = tdot(uv[0], picked)
        parent_down = (both[:RANK, :NRHS] + both[RANK:, NRHS:]).astype(BF)
        lifted = jnp.concatenate([jnp.zeros((RANK, NRHS), BF), parent_down], axis=0)
        down_from_parent[...] = dot(tv[...].reshape(LEAF_DEV * RANK, 2 * RANK), lifted).reshape(
            LEAF_DEV, 4, 16, NRHS
        )

    tall_row = lax.broadcasted_iota(jnp.int32, (256, 256), 0).astype(F32)

    def slots(i, h):
        region = xr.at[i, pl.ds(2 * h, 2), pl.ds(0, 7)]
        pltpu.make_async_copy(region, region, xr_sem.at[i, h]).wait()
        hot = jnp.where(tall_row == vrow[i:i + 1, :], 1.0, 0.0).astype(BF)
        blocks = jnp.concatenate([xr[i, 2 * h + q].reshape(256, NRHS) for q in range(2)], axis=1)
        sums = dot(hot, blocks)
        return [sums[:, q * NRHS:(q + 1) * NRHS] for q in range(2)]

    def z_copy(i, h, sign):
        rows = pl.ds(0, 256) if i else pl.ds(0 if sign > 0 else 128, 128)
        place = 7 if i == 0 and sign < 0 else i
        return pltpu.make_async_remote_copy(
            zs.at[i, h, :, rows],
            zr.at[i, h, :, rows],
            zs_sem.at[place, h],
            zr_sem.at[place, h],
            device_id=up if sign > 0 else low,
            device_id_type=MESH,
        )

    def unit(i, h):
        sums = slots(i, h)
        if i == 0:
            for q in range(2):
                zs[i, h, q] = sums[q].astype(BF)
            z_copy(i, h, 1).start()
            z_copy(i, h, -1).start()
            return
        if i == 7:
            z_copy(5, h, 1).wait_recv()
            z_copy(6, h, -1).wait_recv()
            for q in range(2):
                total = sums[q] + zr[5, h, q].astype(F32) + zr[6, h, q].astype(F32)
                total = total.reshape(LEAF_DEV, 16, NRHS) + down_from_parent[:, 2 * h + q]
                downs[:, 2 * h + q] = total.astype(BF)
            return
        sign = 1 if i % 2 else -1
        before = max(i - 2, 0)
        z_copy(before, h, sign).wait_recv()
        for q in range(2):
            if before:
                zs[i, h, q] = (sums[q] + zr[before, h, q].astype(F32)).astype(BF)
            else:
                met = slice(0, 128) if sign > 0 else slice(128, 256)
                rest = slice(128, 256) if sign > 0 else slice(0, 128)
                zs[i, h, q, met] = (sums[q][met] + zr[0, h, q, met].astype(F32)).astype(BF)
                zs[i, h, q, rest] = sums[q][rest].astype(BF)
        z_copy(i, h, sign).start()

    unit(0, 0)
    unit(0, 1)
    issue(rounds[2])
    for n in range(2):
        halo_copy(n).wait_recv()
    loads[5].wait()
    loads[8].wait()
    done = 0
    for n, chunks in enumerate(rounds[1:4]):
        if n < 2:
            issue(rounds[n + 3])
        for h in range(2):
            for i in chunks:
                unit(i, h)
                if done == 0:
                    parents()
                if done < 8:
                    lax.fori_loop(2 * done, 2 * done + 2, near_step, 0, unroll=True)
                done += 1

    sent = xs.at[pl.ds(0, 7)]
    unit(7, 0)
    unit(7, 1)

    def out_step(s, carry):
        down = downs[s].reshape(RANK, NRHS)
        lifted = jnp.concatenate([jnp.zeros((RANK, NRHS), BF), down], axis=0)
        out[s] = (dot(bv[s], lifted) + near[s]).astype(BF)
        return carry

    lax.fori_loop(0, LEAF_DEV, out_step, 0, unroll=True)

    pltpu.make_async_copy(sent, sent, xs_sem).wait()
    for n in range(2):
        halo_copy(n).wait_send()
    pltpu.make_async_copy(labr.at[pl.ds(0, 7)], labr.at[pl.ds(0, 7)], lab_ss).wait()
    for k in range(1, 4):
        pc_copy(k).wait_send()
    for h in range(2):
        z_copy(0, h, -1).wait_send()
        for i in range(7):
            z_copy(i, h, 1 if i == 0 or i % 2 else -1).wait_send()


def per_device(
    charges, near_src, near_block, bases, transfers, couple, far_dev, far_leaf, upper_couple, upper_src
):
    hbm = pl.BlockSpec(memory_space=pltpu.HBM)
    dma = pltpu.SemaphoreType.DMA
    out = pl.pallas_call(
        kernel,
        name="adjoint",
        out_shape=pltpu.VMEM((LEAF_DEV, LEAF, NRHS), BF),
        in_specs=[hbm] * 10,
        out_specs=pl.BlockSpec(memory_space=pltpu.VMEM),
        scratch_shapes=[
            pltpu.SMEM((FAR, LEAF_DEV), jnp.int32),
            pltpu.SMEM((FAR, LEAF_DEV), jnp.int32),
            pltpu.SMEM((LEAF_DEV, NEAR), jnp.int32),
            pltpu.SMEM((1, KU), jnp.int32),
            pltpu.VMEM((LEAF_DEV + 2 * HALO, LEAF, NRHS), BF),
            pltpu.VMEM((LEAF_DEV, LEAF, NEAR * LEAF), BF),
            pltpu.VMEM((LEAF_DEV, LEAF, 2 * RANK), BF),
            pltpu.VMEM((LEAF_DEV, RANK, 2 * RANK), BF),
            pltpu.VMEM((LEAF_DEV, RANK, FAR * RANK), BF),
            pltpu.VMEM((1, RANK, KU * RANK), BF),
            pltpu.VMEM((LEAF_DEV, RANK, NRHS), BF),
            pltpu.VMEM((PAIRS + 1, 4, 16, NRHS), BF),
            pltpu.VMEM((8, 128), jnp.int32),
            pltpu.SMEM((8, 128), jnp.int32),
            pltpu.VMEM((8, 128), F32),
            pltpu.VMEM((8, 8, 128), F32),
            pltpu.VMEM((8, 8, 4, 32, NRHS), BF),
            pltpu.VMEM((8, 4, 8, 32, NRHS), BF),
            pltpu.VMEM((16, 256), F32),
            pltpu.VMEM((7, 2, 2, 256, NRHS), BF),
            pltpu.VMEM((7, 2, 2, 256, NRHS), BF),
            pltpu.VMEM((RANK, NRHS), BF),
            pltpu.VMEM((3, RANK, NRHS), BF),
            pltpu.VMEM((LEAF_DEV, 4, 16, NRHS), F32),
            pltpu.VMEM((LEAF_DEV, LEAF, NRHS), F32),
            pltpu.VMEM((LEAF_DEV, 4, 16, NRHS), BF),
            dma((10,)),
            dma,
            dma((2,)),
            dma((2,)),
            dma,
            dma,
            dma((3,)),
            dma((3,)),
            dma,
            dma((8, 2)),
            dma((8, 2)),
            dma((8, 2)),
        ],
        compiler_params=pltpu.CompilerParams(
            collective_id=0, has_side_effects=True, vmem_limit_bytes=24 * 1024 * 1024
        ),
    )(
        *[
            pltpu.with_memory_space_constraint(a, pltpu.HBM)
            for a in (
                far_dev.T, far_leaf.T, near_src, upper_src,
                charges.reshape(LEAF_DEV, LEAF, NRHS), near_block, bases, transfers, couple, upper_couple,
            )
        ]
    )
    return out.reshape(LEAF_DEV * LEAF, NRHS)


def solution(mesh):
    rows = P(("branch", "leaf"), None)
    blocks = P(("branch", "leaf"), None, None)
    in_specs = (rows, rows, blocks, blocks, blocks, blocks, rows, rows, blocks, rows)
    return jax.shard_map(per_device, mesh=mesh, in_specs=in_specs, out_specs=rows, check_vma=False)
```

```python
import jax
import jax.numpy as jnp
from jax import lax
from jax.experimental import pallas as pl
from jax.experimental.pallas import tpu as pltpu
from jax.sharding import PartitionSpec as P

LEAF = 64
RANK = 64
NRHS = 128
LEAF_DEV = 16
NEAR = 12
FAR = 3
HALO = 8
KU = 2
PAIRS = LEAF_DEV * FAR
EMPTY = PAIRS * 32 + LEAF_DEV
MESH = pl.DeviceIdType.MESH
BF = jnp.bfloat16
F32 = jnp.float32


def tdot(a, b):
    return lax.dot_general(a, b, (((0,), (0,)), ((), ())), preferred_element_type=F32)


def dot(a, b):
    return jnp.dot(a, b, preferred_element_type=F32)


def step_of(i):
    far = 4 - (i + 1) // 2
    return far if i % 2 == 1 or i == 0 else -far


def kernel(
    fd_hbm, fl_hbm, ns_hbm, us_hbm, charges, near_block, bases, transfers, couple, upper,
    out,
    fd, fl, ns, us, pad, nb, bv, tv, cv, uv, coeff, cpl, idxv, idxs, lab, labr, xs, xr, vrow, zs, zr, pcs, pcr,
    down_from_parent, near, downs,
    load_sem, idx_sem, halo_ss, halo_rs, lab_ss, lab_rs, pc_ss, pc_rs, xs_sem, xr_sem, zs_sem, zr_sem, later_sem,
):
    b = lax.axis_index("branch")
    me = lax.axis_index("leaf")
    c = me % 2
    z = (me // 2) % 8
    x = me // 16
    g = x * 2 + c
    left = (b, (me + 63) % 64)
    right = (b, (me + 1) % 64)
    up = (b, (x * 8 + (z + 1) % 8) * 2 + c)
    low = (b, (x * 8 + (z + 7) % 8) * 2 + c)

    def member(k):
        other = (g + k) % 8
        return other, (b, ((other // 2) * 8 + z) * 2 + other % 2)

    def group(k):
        return ((b + k) % 4, me)

    barrier = pltpu.get_barrier_semaphore()
    partners = [member(k)[1] for k in range(1, 8)] + [up, low, left, right]
    for partner in partners:
        pl.semaphore_signal(barrier, inc=1, device_id=partner, device_id_type=MESH)
    for k in range(1, 4):

        @pl.when(b + k < 4)
        def _():
            pl.semaphore_signal(barrier, inc=1, device_id=group(k), device_id_type=MESH)

    mine = pad.at[pl.ds(HALO, LEAF_DEV)]
    loads = [
        pltpu.make_async_copy(src, dst, load_sem.at[n])
        for n, (src, dst) in enumerate(
            [
                (charges, mine), (bases, bv), (couple, cv), (transfers, tv), (upper, uv), (near_block, nb),
                (fd_hbm, fd), (fl_hbm, fl), (ns_hbm, ns), (us_hbm, us),
            ]
        )
    ]
    for n in (6, 7, 0, 1, 2):
        loads[n].start()

    loads[6].wait()
    loads[7].wait()
    lane = lax.broadcasted_iota(jnp.int32, (8, 128), 1)
    row = lax.broadcasted_iota(jnp.int32, (8, 128), 0)
    one = jnp.full((8, 128), EMPTY, jnp.int32)
    two = jnp.full((8, 128), EMPTY, jnp.int32)
    for t in range(LEAF_DEV):
        for k in range(FAR):
            code = (t * FAR + k) * 32 + fl[k, t]
            hit = lane == fd[k, t]
            taken = one != EMPTY
            two = jnp.where(hit & taken, code, two)
            one = jnp.where(hit & ~taken, code, one)
    code = jnp.where(row == 0, one, jnp.where(row == 1, two, EMPTY))
    idxv[...] = code >> 5
    to_scalars = pltpu.make_async_copy(idxv, idxs, idx_sem)
    to_scalars.start()
    lab[...] = (code & 31).astype(F32)

    loads[0].wait()
    loads[1].wait()

    def coeff_step(t, carry):
        coeff[t] = tdot(bv[t], pad[t + HALO])[:RANK].astype(BF)
        return carry

    lax.fori_loop(0, LEAF_DEV, coeff_step, 0, unroll=True)

    pl.semaphore_wait(barrier, len(partners) + b)
    for k in range(1, 4):

        @pl.when(b + k >= 4)
        def _():
            pl.semaphore_signal(later_sem, inc=1, device_id=group(k), device_id_type=MESH)


    def halo_copy(n):
        src = pad.at[pl.ds(LEAF_DEV if n == 0 else HALO, HALO)]
        dst = pad.at[pl.ds(0 if n == 0 else HALO + LEAF_DEV, HALO)]
        return pltpu.make_async_remote_copy(
            src, dst, halo_ss.at[n], halo_rs.at[n], device_id=(right, left)[n], device_id_type=MESH
        )

    for n in range(2):
        halo_copy(n).start()

    def lab_copy(k):
        return pltpu.make_async_remote_copy(
            lab, labr.at[g], lab_ss, lab_rs, device_id=member(k)[1], device_id_type=MESH
        )

    def lab_step(k, carry):
        lab_copy(k).start()
        return carry

    lax.fori_loop(1, 8, lab_step, 0)
    labr[g] = lab[...]

    loads[2].wait()

    def couple_step(t, carry):
        product = tdot(cv[t], coeff[t]).astype(BF)
        cpl[pl.ds(t * FAR, FAR)] = product.reshape(FAR, 4, 16, NRHS)
        return carry

    lax.fori_loop(0, LEAF_DEV, couple_step, 0, unroll=True)
    cpl[PAIRS] = jnp.zeros((4, 16, NRHS), BF)
    to_scalars.wait()

    def z_of(i):
        return (z + step_of(i) + 8) % 8

    def fill(i):
        def fill_step(other, carry):
            device = ((other // 2) * 8 + z_of(i)) * 2 + other % 2
            for slot in range(2):
                xs[other, i, :, slot * 16:(slot + 1) * 16, :] = cpl[idxs[slot, device]]
            return carry

        lax.fori_loop(0, 8, fill_step, 0, unroll=True)
        xr[i, :, g] = xs[g, i]

    def send_x(i, h):
        def send_step(k, carry):
            other, target = member(k)
            pltpu.make_async_remote_copy(
                xs.at[other, i, pl.ds(2 * h, 2)],
                xr.at[i, pl.ds(2 * h, 2), g],
                xs_sem,
                xr_sem.at[i, h],
                device_id=target,
                device_id_type=MESH,
            ).start()
            return carry

        lax.fori_loop(1, 8, send_step, 0, unroll=True)

    rounds = [(0,), (1, 2), (3, 4), (5, 6), (7,)]

    def issue(chunks):
        for i in chunks:
            fill(i)
        for h in range(2):
            for i in chunks:
                send_x(i, h)

    issue(rounds[0])
    issue(rounds[1])
    for n in (3, 4, 5, 8, 9):
        loads[n].start()

    loads[3].wait()
    packed = tdot(tv[...].reshape(LEAF_DEV * RANK, 2 * RANK), coeff[...].reshape(LEAF_DEV * RANK, NRHS))
    pcs[...] = packed[:RANK].astype(BF)

    def pc_copy(k):
        return pltpu.make_async_remote_copy(
            pcs, pcr.at[3 - k], pc_ss.at[k - 1], pc_rs.at[3 - k], device_id=group(k), device_id_type=MESH
        )

    @pl.when(b < 3)
    def _():
        pl.semaphore_wait(later_sem, 3 - b)

    for k in range(1, 4):
        pc_copy(k).start()

    pltpu.make_async_copy(labr.at[pl.ds(0, 7)], labr.at[pl.ds(0, 7)], lab_rs).wait()
    spread_row = lax.broadcasted_iota(jnp.int32, (64, 256), 0)
    spread_col = lax.broadcasted_iota(jnp.int32, (64, 256), 1)
    spread = (spread_row // 8 == spread_col // 32) & (spread_row % 8 == (spread_col // 16) % 2)
    by_device = tdot(labr[...].reshape(64, 128).astype(BF), spread.astype(F32).astype(BF)).astype(BF)
    chunk = lax.broadcasted_iota(jnp.int32, (16, 128), 0)
    far = 4 - (chunk + 1) // 2
    chunk_z = (z + jnp.where(chunk % 2 == 1, far, -far) + 16) % 8
    pick = lax.broadcasted_iota(jnp.int32, (16, 128), 1) == (x * 8 + chunk_z) * 2 + c
    labels = dot(pick.astype(F32).astype(BF), by_device)
    column = lax.broadcasted_iota(jnp.int32, (16, 256), 1)
    vrow[...] = labels * 16.0 + (column % 16).astype(F32)

    first = (b * 64 + me) * LEAF_DEV - HALO

    def near_step(s, carry):
        tall = jnp.concatenate([nb[s, :, 128 * j:128 * (j + 1)] for j in range(NEAR // 2)], axis=0)
        even = jnp.concatenate([pad[(ns[s, 2 * j] - first) & 31] for j in range(NEAR // 2)], axis=0)
        odd = jnp.concatenate([pad[(ns[s, 2 * j + 1] - first) & 31] for j in range(NEAR // 2)], axis=0)
        both = tdot(tall, jnp.concatenate([even, odd], axis=1))
        near[s] = both[:LEAF, :NRHS] + both[LEAF:, NRHS:]
        return carry

    def parents():
        loads[4].wait()
        loads[9].wait()
        for k in range(1, 4):
            pc_copy(k).wait_recv()
        picked = jnp.concatenate([pcr[jnp.clip(us[0, k] - 1, 0, 2)] for k in range(KU)], axis=1)
        both = tdot(uv[0], picked)
        parent_down = (both[:RANK, :NRHS] + both[RANK:, NRHS:]).astype(BF)
        lifted = jnp.concatenate([jnp.zeros((RANK, NRHS), BF), parent_down], axis=0)
        down_from_parent[...] = dot(tv[...].reshape(LEAF_DEV * RANK, 2 * RANK), lifted).reshape(
            LEAF_DEV, 4, 16, NRHS
        )

    tall_row = lax.broadcasted_iota(jnp.int32, (256, 256), 0).astype(F32)

    def slots(i, h):
        region = xr.at[i, pl.ds(2 * h, 2), pl.ds(0, 7)]
        pltpu.make_async_copy(region, region, xr_sem.at[i, h]).wait()
        hot = jnp.where(tall_row == vrow[i:i + 1, :], 1.0, 0.0).astype(BF)
        blocks = jnp.concatenate([xr[i, 2 * h + q].reshape(256, NRHS) for q in range(2)], axis=1)
        sums = dot(hot, blocks)
        return [sums[:, q * NRHS:(q + 1) * NRHS] for q in range(2)]

    def z_copy(i, h, sign):
        rows = pl.ds(0, 256) if i else pl.ds(0 if sign > 0 else 128, 128)
        place = 7 if i == 0 and sign < 0 else i
        return pltpu.make_async_remote_copy(
            zs.at[i, h, :, rows],
            zr.at[i, h, :, rows],
            zs_sem.at[place, h],
            zr_sem.at[place, h],
            device_id=up if sign > 0 else low,
            device_id_type=MESH,
        )

    def unit(i, h):
        sums = slots(i, h)
        if i == 0:
            for q in range(2):
                zs[i, h, q] = sums[q].astype(BF)
            z_copy(i, h, 1).start()
            z_copy(i, h, -1).start()
            return
        if i == 7:
            z_copy(5, h, 1).wait_recv()
            z_copy(6, h, -1).wait_recv()
            for q in range(2):
                total = sums[q] + zr[5, h, q].astype(F32) + zr[6, h, q].astype(F32)
                total = total.reshape(LEAF_DEV, 16, NRHS) + down_from_parent[:, 2 * h + q]
                downs[:, 2 * h + q] = total.astype(BF)
            return
        sign = 1 if i % 2 else -1
        before = max(i - 2, 0)
        z_copy(before, h, sign).wait_recv()
        for q in range(2):
            if before:
                zs[i, h, q] = (sums[q] + zr[before, h, q].astype(F32)).astype(BF)
            else:
                met = slice(0, 128) if sign > 0 else slice(128, 256)
                rest = slice(128, 256) if sign > 0 else slice(0, 128)
                zs[i, h, q, met] = (sums[q][met] + zr[0, h, q, met].astype(F32)).astype(BF)
                zs[i, h, q, rest] = sums[q][rest].astype(BF)
        z_copy(i, h, sign).start()

    unit(0, 0)
    unit(0, 1)
    issue(rounds[2])
    for n in range(2):
        halo_copy(n).wait_recv()
    loads[5].wait()
    loads[8].wait()
    done = 0
    for n, chunks in enumerate(rounds[1:4]):
        if n < 2:
            issue(rounds[n + 3])
        for h in range(2):
            for i in chunks:
                unit(i, h)
                if done == 0:
                    parents()
                if done < 8:
                    lax.fori_loop(2 * done, 2 * done + 2, near_step, 0, unroll=True)
                done += 1

    sent = xs.at[pl.ds(0, 7)]
    unit(7, 0)
    unit(7, 1)

    def out_step(s, carry):
        down = downs[s].reshape(RANK, NRHS)
        lifted = jnp.concatenate([jnp.zeros((RANK, NRHS), BF), down], axis=0)
        out[s] = (dot(bv[s], lifted) + near[s]).astype(BF)
        return carry

    lax.fori_loop(0, LEAF_DEV, out_step, 0, unroll=True)

    pltpu.make_async_copy(sent, sent, xs_sem).wait()
    for n in range(2):
        halo_copy(n).wait_send()
    pltpu.make_async_copy(labr.at[pl.ds(0, 7)], labr.at[pl.ds(0, 7)], lab_ss).wait()
    for k in range(1, 4):
        pc_copy(k).wait_send()
    for h in range(2):
        z_copy(0, h, -1).wait_send()
        for i in range(7):
            z_copy(i, h, 1 if i == 0 or i % 2 else -1).wait_send()


def per_device(
    charges, near_src, near_block, bases, transfers, couple, far_dev, far_leaf, upper_couple, upper_src
):
    hbm = pl.BlockSpec(memory_space=pltpu.HBM)
    dma = pltpu.SemaphoreType.DMA
    out = pl.pallas_call(
        kernel,
        name="adjoint",
        out_shape=pltpu.VMEM((LEAF_DEV, LEAF, NRHS), BF),
        in_specs=[hbm] * 10,
        out_specs=pl.BlockSpec(memory_space=pltpu.VMEM),
        scratch_shapes=[
            pltpu.SMEM((FAR, LEAF_DEV), jnp.int32),
            pltpu.SMEM((FAR, LEAF_DEV), jnp.int32),
            pltpu.SMEM((LEAF_DEV, NEAR), jnp.int32),
            pltpu.SMEM((1, KU), jnp.int32),
            pltpu.VMEM((LEAF_DEV + 2 * HALO, LEAF, NRHS), BF),
            pltpu.VMEM((LEAF_DEV, LEAF, NEAR * LEAF), BF),
            pltpu.VMEM((LEAF_DEV, LEAF, 2 * RANK), BF),
            pltpu.VMEM((LEAF_DEV, RANK, 2 * RANK), BF),
            pltpu.VMEM((LEAF_DEV, RANK, FAR * RANK), BF),
            pltpu.VMEM((1, RANK, KU * RANK), BF),
            pltpu.VMEM((LEAF_DEV, RANK, NRHS), BF),
            pltpu.VMEM((PAIRS + 1, 4, 16, NRHS), BF),
            pltpu.VMEM((8, 128), jnp.int32),
            pltpu.SMEM((8, 128), jnp.int32),
            pltpu.VMEM((8, 128), F32),
            pltpu.VMEM((8, 8, 128), F32),
            pltpu.VMEM((8, 8, 4, 32, NRHS), BF),
            pltpu.VMEM((8, 4, 8, 32, NRHS), BF),
            pltpu.VMEM((16, 256), F32),
            pltpu.VMEM((7, 2, 2, 256, NRHS), BF),
            pltpu.VMEM((7, 2, 2, 256, NRHS), BF),
            pltpu.VMEM((RANK, NRHS), BF),
            pltpu.VMEM((3, RANK, NRHS), BF),
            pltpu.VMEM((LEAF_DEV, 4, 16, NRHS), F32),
            pltpu.VMEM((LEAF_DEV, LEAF, NRHS), F32),
            pltpu.VMEM((LEAF_DEV, 4, 16, NRHS), BF),
            dma((10,)),
            dma,
            dma((2,)),
            dma((2,)),
            dma,
            dma,
            dma((3,)),
            dma((3,)),
            dma,
            dma((8, 2)),
            dma((8, 2)),
            dma((8, 2)),
            pltpu.SemaphoreType.REGULAR,
        ],
        compiler_params=pltpu.CompilerParams(
            collective_id=0, has_side_effects=True, vmem_limit_bytes=24 * 1024 * 1024
        ),
    )(
        *[
            pltpu.with_memory_space_constraint(a, pltpu.HBM)
            for a in (
                far_dev.T, far_leaf.T, near_src, upper_src,
                charges.reshape(LEAF_DEV, LEAF, NRHS), near_block, bases, transfers, couple, upper_couple,
            )
        ]
    )
    return out.reshape(LEAF_DEV * LEAF, NRHS)


def solution(mesh):
    rows = P(("branch", "leaf"), None)
    blocks = P(("branch", "leaf"), None, None)
    in_specs = (rows, rows, blocks, blocks, blocks, blocks, rows, rows, blocks, rows)
    return jax.shard_map(per_device, mesh=mesh, in_specs=in_specs, out_specs=rows, check_vma=False)
```

```python
import jax
import jax.numpy as jnp
from jax import lax
from jax.experimental import pallas as pl
from jax.experimental.pallas import tpu as pltpu
from jax.sharding import PartitionSpec as P

LEAF = 64
RANK = 64
NRHS = 128
LEAF_DEV = 16
NEAR = 12
FAR = 3
HALO = 8
KU = 2
PAIRS = LEAF_DEV * FAR
EMPTY = PAIRS * 32 + LEAF_DEV
TURNS = [(2, 1), (3, 1), (1, 1), (2, 0), (3, 0), (1, 0), (0, 1)]
MESH = pl.DeviceIdType.MESH
BF = jnp.bfloat16
F32 = jnp.float32


def tdot(a, b):
    return lax.dot_general(a, b, (((0,), (0,)), ((), ())), preferred_element_type=F32)


def dot(a, b):
    return jnp.dot(a, b, preferred_element_type=F32)


def step_of(i):
    far = 4 - (i + 1) // 2
    return far if i % 2 == 1 or i == 0 else -far


def kernel(
    fd_hbm, fl_hbm, ns_hbm, us_hbm, charges, near_block, bases, transfers, couple, upper,
    out,
    fd, fl, ns, us, pad, nb, bv, tv, cv, uv, coeff, cpl, idxv, idxs, lab, labr, xs, xr, vrow, zs, zr, pcs, pcr,
    down_from_parent, near, downs,
    load_sem, idx_sem, halo_ss, halo_rs, lab_ss, lab_rs, pc_ss, pc_rs, xs_sem, xr_sem, zs_sem, zr_sem, later_sem,
):
    b = lax.axis_index("branch")
    me = lax.axis_index("leaf")
    c = me % 2
    z = (me // 2) % 8
    x = me // 16
    g = x * 2 + c
    left = (b, (me + 63) % 64)
    right = (b, (me + 1) % 64)
    up = (b, (x * 8 + (z + 1) % 8) * 2 + c)
    low = (b, (x * 8 + (z + 7) % 8) * 2 + c)

    def member(k):
        ahead, flip = TURNS[k - 1]
        other = ((x + ahead) % 4) * 2 + (c + flip) % 2
        return other, (b, ((other // 2) * 8 + z) * 2 + other % 2)

    def group(k):
        return ((b + k) % 4, me)

    barrier = pltpu.get_barrier_semaphore()
    partners = [member(k)[1] for k in range(1, 8)] + [up, low, left, right]
    for partner in partners:
        pl.semaphore_signal(barrier, inc=1, device_id=partner, device_id_type=MESH)
    for k in range(1, 4):

        @pl.when(b + k < 4)
        def _():
            pl.semaphore_signal(barrier, inc=1, device_id=group(k), device_id_type=MESH)

    mine = pad.at[pl.ds(HALO, LEAF_DEV)]
    loads = [
        pltpu.make_async_copy(src, dst, load_sem.at[n])
        for n, (src, dst) in enumerate(
            [
                (charges, mine), (bases, bv), (couple, cv), (transfers, tv), (upper, uv), (near_block, nb),
                (fd_hbm, fd), (fl_hbm, fl), (ns_hbm, ns), (us_hbm, us),
            ]
        )
    ]
    for n in (6, 7, 0, 1, 2):
        loads[n].start()

    loads[6].wait()
    loads[7].wait()
    lane = lax.broadcasted_iota(jnp.int32, (8, 128), 1)
    row = lax.broadcasted_iota(jnp.int32, (8, 128), 0)
    one = jnp.full((8, 128), EMPTY, jnp.int32)
    two = jnp.full((8, 128), EMPTY, jnp.int32)
    for t in range(LEAF_DEV):
        for k in range(FAR):
            code = (t * FAR + k) * 32 + fl[k, t]
            hit = lane == fd[k, t]
            taken = one != EMPTY
            two = jnp.where(hit & taken, code, two)
            one = jnp.where(hit & ~taken, code, one)
    code = jnp.where(row == 0, one, jnp.where(row == 1, two, EMPTY))
    idxv[...] = code >> 5
    to_scalars = pltpu.make_async_copy(idxv, idxs, idx_sem)
    to_scalars.start()
    lab[...] = (code & 31).astype(F32)

    loads[0].wait()
    loads[1].wait()

    def coeff_step(t, carry):
        coeff[t] = tdot(bv[t], pad[t + HALO])[:RANK].astype(BF)
        return carry

    lax.fori_loop(0, LEAF_DEV, coeff_step, 0, unroll=True)

    pl.semaphore_wait(barrier, len(partners) + b)
    for k in range(1, 4):

        @pl.when(b + k >= 4)
        def _():
            pl.semaphore_signal(later_sem, inc=1, device_id=group(k), device_id_type=MESH)


    def halo_copy(n):
        src = pad.at[pl.ds(LEAF_DEV if n == 0 else HALO, HALO)]
        dst = pad.at[pl.ds(0 if n == 0 else HALO + LEAF_DEV, HALO)]
        return pltpu.make_async_remote_copy(
            src, dst, halo_ss.at[n], halo_rs.at[n], device_id=(right, left)[n], device_id_type=MESH
        )

    for n in range(2):
        halo_copy(n).start()

    def lab_copy(k):
        return pltpu.make_async_remote_copy(
            lab, labr.at[g], lab_ss, lab_rs, device_id=member(k)[1], device_id_type=MESH
        )

    for k in range(1, 8):
        lab_copy(k).start()
    labr[g] = lab[...]

    loads[2].wait()

    def couple_step(t, carry):
        product = tdot(cv[t], coeff[t]).astype(BF)
        cpl[pl.ds(t * FAR, FAR)] = product.reshape(FAR, 4, 16, NRHS)
        return carry

    lax.fori_loop(0, LEAF_DEV, couple_step, 0, unroll=True)
    cpl[PAIRS] = jnp.zeros((4, 16, NRHS), BF)
    to_scalars.wait()

    def z_of(i):
        return (z + step_of(i) + 8) % 8

    def fill(i):
        def fill_step(other, carry):
            device = ((other // 2) * 8 + z_of(i)) * 2 + other % 2
            for slot in range(2):
                xs[other, i, :, slot * 16:(slot + 1) * 16, :] = cpl[idxs[slot, device]]
            return carry

        lax.fori_loop(0, 8, fill_step, 0, unroll=True)
        xr[i, :, g] = xs[g, i]

    def send_x(i, h):
        for k in range(1, 8):
            other, target = member(k)
            pltpu.make_async_remote_copy(
                xs.at[other, i, pl.ds(2 * h, 2)],
                xr.at[i, pl.ds(2 * h, 2), g],
                xs_sem,
                xr_sem.at[i, h],
                device_id=target,
                device_id_type=MESH,
            ).start()

    rounds = [(0,), (1, 2), (3, 4), (5, 6), (7,)]

    def issue(chunks):
        for i in chunks:
            fill(i)
        for h in range(2):
            for i in chunks:
                send_x(i, h)

    issue(rounds[0])
    issue(rounds[1])
    for n in (3, 4, 5, 8, 9):
        loads[n].start()

    loads[3].wait()
    packed = tdot(tv[...].reshape(LEAF_DEV * RANK, 2 * RANK), coeff[...].reshape(LEAF_DEV * RANK, NRHS))
    pcs[...] = packed[:RANK].astype(BF)

    def pc_copy(k):
        return pltpu.make_async_remote_copy(
            pcs, pcr.at[3 - k], pc_ss.at[k - 1], pc_rs.at[3 - k], device_id=group(k), device_id_type=MESH
        )

    @pl.when(b < 3)
    def _():
        pl.semaphore_wait(later_sem, 3 - b)

    for k in range(1, 4):
        pc_copy(k).start()

    pltpu.make_async_copy(labr.at[pl.ds(0, 7)], labr.at[pl.ds(0, 7)], lab_rs).wait()
    spread_row = lax.broadcasted_iota(jnp.int32, (64, 256), 0)
    spread_col = lax.broadcasted_iota(jnp.int32, (64, 256), 1)
    spread = (spread_row // 8 == spread_col // 32) & (spread_row % 8 == (spread_col // 16) % 2)
    by_device = tdot(labr[...].reshape(64, 128).astype(BF), spread.astype(F32).astype(BF)).astype(BF)
    chunk = lax.broadcasted_iota(jnp.int32, (16, 128), 0)
    far = 4 - (chunk + 1) // 2
    chunk_z = (z + jnp.where(chunk % 2 == 1, far, -far) + 16) % 8
    pick = lax.broadcasted_iota(jnp.int32, (16, 128), 1) == (x * 8 + chunk_z) * 2 + c
    labels = dot(pick.astype(F32).astype(BF), by_device)
    column = lax.broadcasted_iota(jnp.int32, (16, 256), 1)
    vrow[...] = labels * 16.0 + (column % 16).astype(F32)

    first = (b * 64 + me) * LEAF_DEV - HALO

    def near_step(s, carry):
        tall = jnp.concatenate([nb[s, :, 128 * j:128 * (j + 1)] for j in range(NEAR // 2)], axis=0)
        even = jnp.concatenate([pad[(ns[s, 2 * j] - first) & 31] for j in range(NEAR // 2)], axis=0)
        odd = jnp.concatenate([pad[(ns[s, 2 * j + 1] - first) & 31] for j in range(NEAR // 2)], axis=0)
        both = tdot(tall, jnp.concatenate([even, odd], axis=1))
        near[s] = both[:LEAF, :NRHS] + both[LEAF:, NRHS:]
        return carry

    def parents():
        loads[4].wait()
        loads[9].wait()
        for k in range(1, 4):
            pc_copy(k).wait_recv()
        picked = jnp.concatenate([pcr[jnp.clip(us[0, k] - 1, 0, 2)] for k in range(KU)], axis=1)
        both = tdot(uv[0], picked)
        parent_down = (both[:RANK, :NRHS] + both[RANK:, NRHS:]).astype(BF)
        lifted = jnp.concatenate([jnp.zeros((RANK, NRHS), BF), parent_down], axis=0)
        down_from_parent[...] = dot(tv[...].reshape(LEAF_DEV * RANK, 2 * RANK), lifted).reshape(
            LEAF_DEV, 4, 16, NRHS
        )

    tall_row = lax.broadcasted_iota(jnp.int32, (256, 256), 0).astype(F32)

    def slots(i, h):
        region = xr.at[i, pl.ds(2 * h, 2), pl.ds(0, 7)]
        pltpu.make_async_copy(region, region, xr_sem.at[i, h]).wait()
        hot = jnp.where(tall_row == vrow[i:i + 1, :], 1.0, 0.0).astype(BF)
        blocks = jnp.concatenate([xr[i, 2 * h + q].reshape(256, NRHS) for q in range(2)], axis=1)
        sums = dot(hot, blocks)
        return [sums[:, q * NRHS:(q + 1) * NRHS] for q in range(2)]

    def z_copy(i, h, sign):
        rows = pl.ds(0, 256) if i else pl.ds(0 if sign > 0 else 128, 128)
        place = 7 if i == 0 and sign < 0 else i
        return pltpu.make_async_remote_copy(
            zs.at[i, h, :, rows],
            zr.at[i, h, :, rows],
            zs_sem.at[place, h],
            zr_sem.at[place, h],
            device_id=up if sign > 0 else low,
            device_id_type=MESH,
        )

    def unit(i, h):
        sums = slots(i, h)
        if i == 0:
            for q in range(2):
                zs[i, h, q] = sums[q].astype(BF)
            z_copy(i, h, 1).start()
            z_copy(i, h, -1).start()
            return
        if i == 7:
            z_copy(5, h, 1).wait_recv()
            z_copy(6, h, -1).wait_recv()
            for q in range(2):
                total = sums[q] + zr[5, h, q].astype(F32) + zr[6, h, q].astype(F32)
                total = total.reshape(LEAF_DEV, 16, NRHS) + down_from_parent[:, 2 * h + q]
                downs[:, 2 * h + q] = total.astype(BF)
            return
        sign = 1 if i % 2 else -1
        before = max(i - 2, 0)
        z_copy(before, h, sign).wait_recv()
        for q in range(2):
            if before:
                zs[i, h, q] = (sums[q] + zr[before, h, q].astype(F32)).astype(BF)
            else:
                met = slice(0, 128) if sign > 0 else slice(128, 256)
                rest = slice(128, 256) if sign > 0 else slice(0, 128)
                zs[i, h, q, met] = (sums[q][met] + zr[0, h, q, met].astype(F32)).astype(BF)
                zs[i, h, q, rest] = sums[q][rest].astype(BF)
        z_copy(i, h, sign).start()

    unit(0, 0)
    unit(0, 1)
    issue(rounds[2])
    for n in range(2):
        halo_copy(n).wait_recv()
    loads[5].wait()
    loads[8].wait()
    done = 0
    for n, chunks in enumerate(rounds[1:4]):
        if n < 2:
            issue(rounds[n + 3])
        for h in range(2):
            for i in chunks:
                unit(i, h)
                if done == 0:
                    parents()
                if done < 8:
                    lax.fori_loop(2 * done, 2 * done + 2, near_step, 0, unroll=True)
                done += 1

    sent = xs.at[pl.ds(0, 7)]
    unit(7, 0)
    unit(7, 1)

    def out_step(s, carry):
        down = downs[s].reshape(RANK, NRHS)
        lifted = jnp.concatenate([jnp.zeros((RANK, NRHS), BF), down], axis=0)
        out[s] = (dot(bv[s], lifted) + near[s]).astype(BF)
        return carry

    lax.fori_loop(0, LEAF_DEV, out_step, 0, unroll=True)

    pltpu.make_async_copy(sent, sent, xs_sem).wait()
    for n in range(2):
        halo_copy(n).wait_send()
    pltpu.make_async_copy(labr.at[pl.ds(0, 7)], labr.at[pl.ds(0, 7)], lab_ss).wait()
    for k in range(1, 4):
        pc_copy(k).wait_send()
    for h in range(2):
        z_copy(0, h, -1).wait_send()
        for i in range(7):
            z_copy(i, h, 1 if i == 0 or i % 2 else -1).wait_send()


def per_device(
    charges, near_src, near_block, bases, transfers, couple, far_dev, far_leaf, upper_couple, upper_src
):
    hbm = pl.BlockSpec(memory_space=pltpu.HBM)
    dma = pltpu.SemaphoreType.DMA
    out = pl.pallas_call(
        kernel,
        name="adjoint",
        out_shape=pltpu.VMEM((LEAF_DEV, LEAF, NRHS), BF),
        in_specs=[hbm] * 10,
        out_specs=pl.BlockSpec(memory_space=pltpu.VMEM),
        scratch_shapes=[
            pltpu.SMEM((FAR, LEAF_DEV), jnp.int32),
            pltpu.SMEM((FAR, LEAF_DEV), jnp.int32),
            pltpu.SMEM((LEAF_DEV, NEAR), jnp.int32),
            pltpu.SMEM((1, KU), jnp.int32),
            pltpu.VMEM((LEAF_DEV + 2 * HALO, LEAF, NRHS), BF),
            pltpu.VMEM((LEAF_DEV, LEAF, NEAR * LEAF), BF),
            pltpu.VMEM((LEAF_DEV, LEAF, 2 * RANK), BF),
            pltpu.VMEM((LEAF_DEV, RANK, 2 * RANK), BF),
            pltpu.VMEM((LEAF_DEV, RANK, FAR * RANK), BF),
            pltpu.VMEM((1, RANK, KU * RANK), BF),
            pltpu.VMEM((LEAF_DEV, RANK, NRHS), BF),
            pltpu.VMEM((PAIRS + 1, 4, 16, NRHS), BF),
            pltpu.VMEM((8, 128), jnp.int32),
            pltpu.SMEM((8, 128), jnp.int32),
            pltpu.VMEM((8, 128), F32),
            pltpu.VMEM((8, 8, 128), F32),
            pltpu.VMEM((8, 8, 4, 32, NRHS), BF),
            pltpu.VMEM((8, 4, 8, 32, NRHS), BF),
            pltpu.VMEM((16, 256), F32),
            pltpu.VMEM((7, 2, 2, 256, NRHS), BF),
            pltpu.VMEM((7, 2, 2, 256, NRHS), BF),
            pltpu.VMEM((RANK, NRHS), BF),
            pltpu.VMEM((3, RANK, NRHS), BF),
            pltpu.VMEM((LEAF_DEV, 4, 16, NRHS), F32),
            pltpu.VMEM((LEAF_DEV, LEAF, NRHS), F32),
            pltpu.VMEM((LEAF_DEV, 4, 16, NRHS), BF),
            dma((10,)),
            dma,
            dma((2,)),
            dma((2,)),
            dma,
            dma,
            dma((3,)),
            dma((3,)),
            dma,
            dma((8, 2)),
            dma((8, 2)),
            dma((8, 2)),
            pltpu.SemaphoreType.REGULAR,
        ],
        compiler_params=pltpu.CompilerParams(
            collective_id=0, has_side_effects=True, vmem_limit_bytes=24 * 1024 * 1024
        ),
    )(
        *[
            pltpu.with_memory_space_constraint(a, pltpu.HBM)
            for a in (
                far_dev.T, far_leaf.T, near_src, upper_src,
                charges.reshape(LEAF_DEV, LEAF, NRHS), near_block, bases, transfers, couple, upper_couple,
            )
        ]
    )
    return out.reshape(LEAF_DEV * LEAF, NRHS)


def solution(mesh):
    rows = P(("branch", "leaf"), None)
    blocks = P(("branch", "leaf"), None, None)
    in_specs = (rows, rows, blocks, blocks, blocks, blocks, rows, rows, blocks, rows)
    return jax.shard_map(per_device, mesh=mesh, in_specs=in_specs, out_specs=rows, check_vma=False)
```

```python
import jax
import jax.numpy as jnp
from jax import lax
from jax.experimental import pallas as pl
from jax.experimental.pallas import tpu as pltpu
from jax.sharding import PartitionSpec as P

LEAF = 64
RANK = 64
NRHS = 128
LEAF_DEV = 16
NEAR = 12
FAR = 3
HALO = 8
KU = 2
PAIRS = LEAF_DEV * FAR
EMPTY = PAIRS * 32 + LEAF_DEV
TURNS = [(2, 1), (3, 1), (1, 1), (2, 0), (3, 0), (1, 0), (0, 1)]
MESH = pl.DeviceIdType.MESH
BF = jnp.bfloat16
F32 = jnp.float32


def tdot(a, b):
    return lax.dot_general(a, b, (((0,), (0,)), ((), ())), preferred_element_type=F32)


def dot(a, b):
    return jnp.dot(a, b, preferred_element_type=F32)


def step_of(i):
    far = 4 - (i + 1) // 2
    return far if i % 2 == 1 or i == 0 else -far


def kernel(
    fd_hbm, fl_hbm, ns_hbm, us_hbm, charges, near_block, bases, transfers, couple, upper,
    out,
    fd, fl, ns, us, pad, nb, bv, tv, cv, uv, coeff, cpl, idxv, idxs, lab, labr, xs, xr, vrow, zs, zr, pcs, pcr,
    down_from_parent, near, downs,
    load_sem, idx_sem, halo_ss, halo_rs, lab_ss, lab_rs, pc_ss, pc_rs, xs_sem, xr_sem, zs_sem, zr_sem, later_sem,
):
    b = lax.axis_index("branch")
    me = lax.axis_index("leaf")
    c = me % 2
    z = (me // 2) % 8
    x = me // 16
    g = x * 2 + c
    left = (b, (me + 63) % 64)
    right = (b, (me + 1) % 64)
    up = (b, (x * 8 + (z + 1) % 8) * 2 + c)
    low = (b, (x * 8 + (z + 7) % 8) * 2 + c)

    def member(k):
        ahead, flip = TURNS[k - 1]
        other = ((x + ahead) % 4) * 2 + (c + flip) % 2
        return other, (b, ((other // 2) * 8 + z) * 2 + other % 2)

    def group(k):
        return ((b + k) % 4, me)

    barrier = pltpu.get_barrier_semaphore()
    partners = [member(k)[1] for k in range(1, 8)] + [up, low, left, right]
    for partner in partners:
        pl.semaphore_signal(barrier, inc=1, device_id=partner, device_id_type=MESH)
    for k in range(1, 4):

        @pl.when(b + k < 4)
        def _():
            pl.semaphore_signal(barrier, inc=1, device_id=group(k), device_id_type=MESH)

    mine = pad.at[pl.ds(HALO, LEAF_DEV)]
    loads = [
        pltpu.make_async_copy(src, dst, load_sem.at[n])
        for n, (src, dst) in enumerate(
            [
                (charges, mine), (bases, bv), (couple, cv), (transfers, tv), (upper, uv), (near_block, nb),
                (fd_hbm, fd), (fl_hbm, fl), (ns_hbm, ns), (us_hbm, us),
            ]
        )
    ]
    for n in (6, 7, 0, 1, 2):
        loads[n].start()

    loads[6].wait()
    loads[7].wait()
    lane = lax.broadcasted_iota(jnp.int32, (8, 128), 1)
    row = lax.broadcasted_iota(jnp.int32, (8, 128), 0)
    one = jnp.full((8, 128), EMPTY, jnp.int32)
    two = jnp.full((8, 128), EMPTY, jnp.int32)
    for t in range(LEAF_DEV):
        for k in range(FAR):
            code = (t * FAR + k) * 32 + fl[k, t]
            hit = lane == fd[k, t]
            taken = one != EMPTY
            two = jnp.where(hit & taken, code, two)
            one = jnp.where(hit & ~taken, code, one)
    code = jnp.where(row == 0, one, jnp.where(row == 1, two, EMPTY))
    idxv[...] = code >> 5
    to_scalars = pltpu.make_async_copy(idxv, idxs, idx_sem)
    to_scalars.start()
    lab[...] = (code & 31).astype(F32)

    loads[0].wait()
    loads[1].wait()

    def coeff_step(t, carry):
        coeff[t] = tdot(bv[t], pad[t + HALO])[:RANK].astype(BF)
        return carry

    lax.fori_loop(0, LEAF_DEV, coeff_step, 0, unroll=True)

    pl.semaphore_wait(barrier, len(partners) + b)
    for k in range(1, 4):

        @pl.when(b + k >= 4)
        def _():
            pl.semaphore_signal(later_sem, inc=1, device_id=group(k), device_id_type=MESH)


    def halo_copy(n):
        src = pad.at[pl.ds(LEAF_DEV if n == 0 else HALO, HALO)]
        dst = pad.at[pl.ds(0 if n == 0 else HALO + LEAF_DEV, HALO)]
        return pltpu.make_async_remote_copy(
            src, dst, halo_ss.at[n], halo_rs.at[n], device_id=(right, left)[n], device_id_type=MESH
        )


    def lab_copy(k):
        return pltpu.make_async_remote_copy(
            lab, labr.at[g], lab_ss, lab_rs, device_id=member(k)[1], device_id_type=MESH
        )

    for k in range(1, 8):
        lab_copy(k).start()
    for n in range(2):
        halo_copy(n).start()
    labr[g] = lab[...]

    loads[2].wait()

    def couple_step(t, carry):
        product = tdot(cv[t], coeff[t]).astype(BF)
        cpl[pl.ds(t * FAR, FAR)] = product.reshape(FAR, 4, 16, NRHS)
        return carry

    lax.fori_loop(0, LEAF_DEV, couple_step, 0, unroll=True)
    cpl[PAIRS] = jnp.zeros((4, 16, NRHS), BF)
    to_scalars.wait()

    def z_of(i):
        return (z + step_of(i) + 8) % 8

    def fill(i):
        def fill_step(other, carry):
            device = ((other // 2) * 8 + z_of(i)) * 2 + other % 2
            for slot in range(2):
                xs[other, i, :, slot * 16:(slot + 1) * 16, :] = cpl[idxs[slot, device]]
            return carry

        lax.fori_loop(0, 8, fill_step, 0, unroll=True)
        xr[i, :, g] = xs[g, i]

    def send_x(i, h):
        for k in range(1, 8):
            other, target = member(k)
            pltpu.make_async_remote_copy(
                xs.at[other, i, pl.ds(2 * h, 2)],
                xr.at[i, pl.ds(2 * h, 2), g],
                xs_sem,
                xr_sem.at[i, h],
                device_id=target,
                device_id_type=MESH,
            ).start()

    rounds = [(0,), (1, 2), (3, 4), (5, 6), (7,)]

    def issue(chunks):
        for i in chunks:
            fill(i)
        for h in range(2):
            for i in chunks:
                send_x(i, h)

    issue(rounds[0])
    issue(rounds[1])
    for n in (3, 4, 5, 8, 9):
        loads[n].start()

    loads[3].wait()
    packed = tdot(tv[...].reshape(LEAF_DEV * RANK, 2 * RANK), coeff[...].reshape(LEAF_DEV * RANK, NRHS))
    pcs[...] = packed[:RANK].astype(BF)

    def pc_copy(k):
        return pltpu.make_async_remote_copy(
            pcs, pcr.at[3 - k], pc_ss.at[k - 1], pc_rs.at[3 - k], device_id=group(k), device_id_type=MESH
        )

    @pl.when(b < 3)
    def _():
        pl.semaphore_wait(later_sem, 3 - b)

    for k in range(1, 4):
        pc_copy(k).start()

    pltpu.make_async_copy(labr.at[pl.ds(0, 7)], labr.at[pl.ds(0, 7)], lab_rs).wait()
    spread_row = lax.broadcasted_iota(jnp.int32, (64, 256), 0)
    spread_col = lax.broadcasted_iota(jnp.int32, (64, 256), 1)
    spread = (spread_row // 8 == spread_col // 32) & (spread_row % 8 == (spread_col // 16) % 2)
    by_device = tdot(labr[...].reshape(64, 128).astype(BF), spread.astype(F32).astype(BF)).astype(BF)
    chunk = lax.broadcasted_iota(jnp.int32, (16, 128), 0)
    far = 4 - (chunk + 1) // 2
    chunk_z = (z + jnp.where(chunk % 2 == 1, far, -far) + 16) % 8
    pick = lax.broadcasted_iota(jnp.int32, (16, 128), 1) == (x * 8 + chunk_z) * 2 + c
    labels = dot(pick.astype(F32).astype(BF), by_device)
    column = lax.broadcasted_iota(jnp.int32, (16, 256), 1)
    vrow[...] = labels * 16.0 + (column % 16).astype(F32)

    first = (b * 64 + me) * LEAF_DEV - HALO

    def near_step(s, carry):
        tall = jnp.concatenate([nb[s, :, 128 * j:128 * (j + 1)] for j in range(NEAR // 2)], axis=0)
        even = jnp.concatenate([pad[(ns[s, 2 * j] - first) & 31] for j in range(NEAR // 2)], axis=0)
        odd = jnp.concatenate([pad[(ns[s, 2 * j + 1] - first) & 31] for j in range(NEAR // 2)], axis=0)
        both = tdot(tall, jnp.concatenate([even, odd], axis=1))
        near[s] = both[:LEAF, :NRHS] + both[LEAF:, NRHS:]
        return carry

    def parents():
        loads[4].wait()
        loads[9].wait()
        for k in range(1, 4):
            pc_copy(k).wait_recv()
        picked = jnp.concatenate([pcr[jnp.clip(us[0, k] - 1, 0, 2)] for k in range(KU)], axis=1)
        both = tdot(uv[0], picked)
        parent_down = (both[:RANK, :NRHS] + both[RANK:, NRHS:]).astype(BF)
        lifted = jnp.concatenate([jnp.zeros((RANK, NRHS), BF), parent_down], axis=0)
        down_from_parent[...] = dot(tv[...].reshape(LEAF_DEV * RANK, 2 * RANK), lifted).reshape(
            LEAF_DEV, 4, 16, NRHS
        )

    tall_row = lax.broadcasted_iota(jnp.int32, (256, 256), 0).astype(F32)

    def slots(i, h):
        region = xr.at[i, pl.ds(2 * h, 2), pl.ds(0, 7)]
        pltpu.make_async_copy(region, region, xr_sem.at[i, h]).wait()
        hot = jnp.where(tall_row == vrow[i:i + 1, :], 1.0, 0.0).astype(BF)
        blocks = jnp.concatenate([xr[i, 2 * h + q].reshape(256, NRHS) for q in range(2)], axis=1)
        sums = dot(hot, blocks)
        return [sums[:, q * NRHS:(q + 1) * NRHS] for q in range(2)]

    def z_copy(i, h, sign):
        rows = pl.ds(0, 256) if i else pl.ds(0 if sign > 0 else 128, 128)
        place = 7 if i == 0 and sign < 0 else i
        return pltpu.make_async_remote_copy(
            zs.at[i, h, :, rows],
            zr.at[i, h, :, rows],
            zs_sem.at[place, h],
            zr_sem.at[place, h],
            device_id=up if sign > 0 else low,
            device_id_type=MESH,
        )

    def unit(i, h):
        sums = slots(i, h)
        if i == 0:
            for q in range(2):
                zs[i, h, q] = sums[q].astype(BF)
            z_copy(i, h, 1).start()
            z_copy(i, h, -1).start()
            return
        if i == 7:
            z_copy(5, h, 1).wait_recv()
            z_copy(6, h, -1).wait_recv()
            for q in range(2):
                total = sums[q] + zr[5, h, q].astype(F32) + zr[6, h, q].astype(F32)
                total = total.reshape(LEAF_DEV, 16, NRHS) + down_from_parent[:, 2 * h + q]
                downs[:, 2 * h + q] = total.astype(BF)
            return
        sign = 1 if i % 2 else -1
        before = max(i - 2, 0)
        z_copy(before, h, sign).wait_recv()
        for q in range(2):
            if before:
                zs[i, h, q] = (sums[q] + zr[before, h, q].astype(F32)).astype(BF)
            else:
                met = slice(0, 128) if sign > 0 else slice(128, 256)
                rest = slice(128, 256) if sign > 0 else slice(0, 128)
                zs[i, h, q, met] = (sums[q][met] + zr[0, h, q, met].astype(F32)).astype(BF)
                zs[i, h, q, rest] = sums[q][rest].astype(BF)
        z_copy(i, h, sign).start()

    unit(0, 0)
    unit(0, 1)
    issue(rounds[2])
    for n in range(2):
        halo_copy(n).wait_recv()
    loads[5].wait()
    loads[8].wait()
    done = 0
    for n, chunks in enumerate(rounds[1:4]):
        if n < 2:
            issue(rounds[n + 3])
        for h in range(2):
            for i in chunks:
                unit(i, h)
                if done == 0:
                    parents()
                if done < 8:
                    lax.fori_loop(2 * done, 2 * done + 2, near_step, 0, unroll=True)
                done += 1

    sent = xs.at[pl.ds(0, 7)]
    unit(7, 0)
    unit(7, 1)

    nothing = jnp.zeros((RANK, NRHS), BF)

    def out_step(s, carry):
        pair = [jnp.concatenate([nothing, downs[2 * s + n].reshape(RANK, NRHS)], axis=0) for n in range(2)]
        both = dot(bv[pl.ds(2 * s, 2)].reshape(2 * LEAF, 2 * RANK), jnp.concatenate(pair, axis=1))
        out[2 * s] = (both[:LEAF, :NRHS] + near[2 * s]).astype(BF)
        out[2 * s + 1] = (both[LEAF:, NRHS:] + near[2 * s + 1]).astype(BF)
        return carry

    lax.fori_loop(0, LEAF_DEV // 2, out_step, 0, unroll=True)

    pltpu.make_async_copy(sent, sent, xs_sem).wait()
    for n in range(2):
        halo_copy(n).wait_send()
    pltpu.make_async_copy(labr.at[pl.ds(0, 7)], labr.at[pl.ds(0, 7)], lab_ss).wait()
    for k in range(1, 4):
        pc_copy(k).wait_send()
    for h in range(2):
        z_copy(0, h, -1).wait_send()
        for i in range(7):
            z_copy(i, h, 1 if i == 0 or i % 2 else -1).wait_send()


def per_device(
    charges, near_src, near_block, bases, transfers, couple, far_dev, far_leaf, upper_couple, upper_src
):
    hbm = pl.BlockSpec(memory_space=pltpu.HBM)
    dma = pltpu.SemaphoreType.DMA
    out = pl.pallas_call(
        kernel,
        name="adjoint",
        out_shape=pltpu.VMEM((LEAF_DEV, LEAF, NRHS), BF),
        in_specs=[hbm] * 10,
        out_specs=pl.BlockSpec(memory_space=pltpu.VMEM),
        scratch_shapes=[
            pltpu.SMEM((FAR, LEAF_DEV), jnp.int32),
            pltpu.SMEM((FAR, LEAF_DEV), jnp.int32),
            pltpu.SMEM((LEAF_DEV, NEAR), jnp.int32),
            pltpu.SMEM((1, KU), jnp.int32),
            pltpu.VMEM((LEAF_DEV + 2 * HALO, LEAF, NRHS), BF),
            pltpu.VMEM((LEAF_DEV, LEAF, NEAR * LEAF), BF),
            pltpu.VMEM((LEAF_DEV, LEAF, 2 * RANK), BF),
            pltpu.VMEM((LEAF_DEV, RANK, 2 * RANK), BF),
            pltpu.VMEM((LEAF_DEV, RANK, FAR * RANK), BF),
            pltpu.VMEM((1, RANK, KU * RANK), BF),
            pltpu.VMEM((LEAF_DEV, RANK, NRHS), BF),
            pltpu.VMEM((PAIRS + 1, 4, 16, NRHS), BF),
            pltpu.VMEM((8, 128), jnp.int32),
            pltpu.SMEM((8, 128), jnp.int32),
            pltpu.VMEM((8, 128), F32),
            pltpu.VMEM((8, 8, 128), F32),
            pltpu.VMEM((8, 8, 4, 32, NRHS), BF),
            pltpu.VMEM((8, 4, 8, 32, NRHS), BF),
            pltpu.VMEM((16, 256), F32),
            pltpu.VMEM((7, 2, 2, 256, NRHS), BF),
            pltpu.VMEM((7, 2, 2, 256, NRHS), BF),
            pltpu.VMEM((RANK, NRHS), BF),
            pltpu.VMEM((3, RANK, NRHS), BF),
            pltpu.VMEM((LEAF_DEV, 4, 16, NRHS), F32),
            pltpu.VMEM((LEAF_DEV, LEAF, NRHS), F32),
            pltpu.VMEM((LEAF_DEV, 4, 16, NRHS), BF),
            dma((10,)),
            dma,
            dma((2,)),
            dma((2,)),
            dma,
            dma,
            dma((3,)),
            dma((3,)),
            dma,
            dma((8, 2)),
            dma((8, 2)),
            dma((8, 2)),
            pltpu.SemaphoreType.REGULAR,
        ],
        compiler_params=pltpu.CompilerParams(
            collective_id=0, has_side_effects=True, vmem_limit_bytes=24 * 1024 * 1024
        ),
    )(
        *[
            pltpu.with_memory_space_constraint(a, pltpu.HBM)
            for a in (
                far_dev.T, far_leaf.T, near_src, upper_src,
                charges.reshape(LEAF_DEV, LEAF, NRHS), near_block, bases, transfers, couple, upper_couple,
            )
        ]
    )
    return out.reshape(LEAF_DEV * LEAF, NRHS)


def solution(mesh):
    rows = P(("branch", "leaf"), None)
    blocks = P(("branch", "leaf"), None, None)
    in_specs = (rows, rows, blocks, blocks, blocks, blocks, rows, rows, blocks, rows)
    return jax.shard_map(per_device, mesh=mesh, in_specs=in_specs, out_specs=rows, check_vma=False)
```

```python
import jax
import jax.numpy as jnp
from jax import lax
from jax.experimental import pallas as pl
from jax.experimental.pallas import tpu as pltpu
from jax.sharding import PartitionSpec as P

LEAF = 64
RANK = 64
NRHS = 128
LEAF_DEV = 16
NEAR = 12
FAR = 3
HALO = 8
KU = 2
PAIRS = LEAF_DEV * FAR
EMPTY = PAIRS * 32 + LEAF_DEV
TURNS = [(2, 1), (3, 1), (1, 1), (2, 0), (3, 0), (1, 0), (0, 1)]
MESH = pl.DeviceIdType.MESH
BF = jnp.bfloat16
F32 = jnp.float32


def tdot(a, b):
    return lax.dot_general(a, b, (((0,), (0,)), ((), ())), preferred_element_type=F32)


def dot(a, b):
    return jnp.dot(a, b, preferred_element_type=F32)


def step_of(i):
    far = 4 - (i + 1) // 2
    return far if i % 2 == 1 or i == 0 else -far


def kernel(
    fd_hbm, fl_hbm, ns_hbm, us_hbm, charges, near_block, bases, transfers, couple, upper,
    out,
    fd, fl, ns, us, pad, nb, bv, tv, cv, uv, coeff, cpl, idxv, idxs, lab, labr, xs, xr, vrow, hots, zs, zr, pcs, pcr,
    down_from_parent, near, downs,
    load_sem, idx_sem, halo_ss, halo_rs, lab_ss, lab_rs, pc_ss, pc_rs, xs_sem, xr_sem, zs_sem, zr_sem, later_sem,
):
    b = lax.axis_index("branch")
    me = lax.axis_index("leaf")
    c = me % 2
    z = (me // 2) % 8
    x = me // 16
    g = x * 2 + c
    left = (b, (me + 63) % 64)
    right = (b, (me + 1) % 64)
    up = (b, (x * 8 + (z + 1) % 8) * 2 + c)
    low = (b, (x * 8 + (z + 7) % 8) * 2 + c)

    def member(k):
        ahead, flip = TURNS[k - 1]
        other = ((x + ahead) % 4) * 2 + (c + flip) % 2
        return other, (b, ((other // 2) * 8 + z) * 2 + other % 2)

    def group(k):
        return ((b + k) % 4, me)

    barrier = pltpu.get_barrier_semaphore()
    partners = [member(k)[1] for k in range(1, 8)] + [up, low, left, right]
    for partner in partners:
        pl.semaphore_signal(barrier, inc=1, device_id=partner, device_id_type=MESH)
    for k in range(1, 4):

        @pl.when(b + k < 4)
        def _():
            pl.semaphore_signal(barrier, inc=1, device_id=group(k), device_id_type=MESH)

    mine = pad.at[pl.ds(HALO, LEAF_DEV)]
    loads = [
        pltpu.make_async_copy(src, dst, load_sem.at[n])
        for n, (src, dst) in enumerate(
            [
                (charges, mine), (bases, bv), (couple, cv), (transfers, tv), (upper, uv), (near_block, nb),
                (fd_hbm, fd), (fl_hbm, fl), (ns_hbm, ns), (us_hbm, us),
            ]
        )
    ]
    for n in (6, 7, 0, 1, 2):
        loads[n].start()

    loads[6].wait()
    loads[7].wait()
    lane = lax.broadcasted_iota(jnp.int32, (8, 128), 1)
    row = lax.broadcasted_iota(jnp.int32, (8, 128), 0)
    one = jnp.full((8, 128), EMPTY, jnp.int32)
    two = jnp.full((8, 128), EMPTY, jnp.int32)
    for t in range(LEAF_DEV):
        for k in range(FAR):
            code = (t * FAR + k) * 32 + fl[k, t]
            hit = lane == fd[k, t]
            taken = one != EMPTY
            two = jnp.where(hit & taken, code, two)
            one = jnp.where(hit & ~taken, code, one)
    code = jnp.where(row == 0, one, jnp.where(row == 1, two, EMPTY))
    idxv[...] = code >> 5
    to_scalars = pltpu.make_async_copy(idxv, idxs, idx_sem)
    to_scalars.start()
    lab[...] = (code & 31).astype(F32)

    loads[0].wait()
    loads[1].wait()

    def coeff_step(t, carry):
        coeff[t] = tdot(bv[t], pad[t + HALO])[:RANK].astype(BF)
        return carry

    lax.fori_loop(0, LEAF_DEV, coeff_step, 0, unroll=True)

    pl.semaphore_wait(barrier, len(partners) + b)
    for k in range(1, 4):

        @pl.when(b + k >= 4)
        def _():
            pl.semaphore_signal(later_sem, inc=1, device_id=group(k), device_id_type=MESH)


    def halo_copy(n):
        src = pad.at[pl.ds(LEAF_DEV if n == 0 else HALO, HALO)]
        dst = pad.at[pl.ds(0 if n == 0 else HALO + LEAF_DEV, HALO)]
        return pltpu.make_async_remote_copy(
            src, dst, halo_ss.at[n], halo_rs.at[n], device_id=(right, left)[n], device_id_type=MESH
        )


    def lab_copy(k):
        return pltpu.make_async_remote_copy(
            lab, labr.at[g], lab_ss, lab_rs, device_id=member(k)[1], device_id_type=MESH
        )

    for k in range(1, 8):
        lab_copy(k).start()
    for n in range(2):
        halo_copy(n).start()
    labr[g] = lab[...]

    loads[2].wait()

    def couple_step(t, carry):
        product = tdot(cv[t], coeff[t]).astype(BF)
        cpl[pl.ds(t * FAR, FAR)] = product.reshape(FAR, 4, 16, NRHS)
        return carry

    lax.fori_loop(0, LEAF_DEV, couple_step, 0, unroll=True)
    cpl[PAIRS] = jnp.zeros((4, 16, NRHS), BF)
    to_scalars.wait()

    def z_of(i):
        return (z + step_of(i) + 8) % 8

    def fill(i):
        def fill_step(other, carry):
            device = ((other // 2) * 8 + z_of(i)) * 2 + other % 2
            for slot in range(2):
                xs[other, i, :, slot * 16:(slot + 1) * 16, :] = cpl[idxs[slot, device]]
            return carry

        lax.fori_loop(0, 8, fill_step, 0, unroll=True)
        xr[i, :, g] = xs[g, i]

    def send_x(i, h):
        for k in range(1, 8):
            other, target = member(k)
            pltpu.make_async_remote_copy(
                xs.at[other, i, pl.ds(2 * h, 2)],
                xr.at[i, pl.ds(2 * h, 2), g],
                xs_sem,
                xr_sem.at[i, h],
                device_id=target,
                device_id_type=MESH,
            ).start()

    rounds = [(0,), (1, 2), (3, 4), (5, 6), (7,)]

    def issue(chunks):
        for i in chunks:
            fill(i)
        for h in range(2):
            for i in chunks:
                send_x(i, h)

    issue(rounds[0])
    issue(rounds[1])
    for n in (3, 4, 5, 8, 9):
        loads[n].start()

    loads[3].wait()
    packed = tdot(tv[...].reshape(LEAF_DEV * RANK, 2 * RANK), coeff[...].reshape(LEAF_DEV * RANK, NRHS))
    pcs[...] = packed[:RANK].astype(BF)

    def pc_copy(k):
        return pltpu.make_async_remote_copy(
            pcs, pcr.at[3 - k], pc_ss.at[k - 1], pc_rs.at[3 - k], device_id=group(k), device_id_type=MESH
        )

    @pl.when(b < 3)
    def _():
        pl.semaphore_wait(later_sem, 3 - b)

    for k in range(1, 4):
        pc_copy(k).start()

    pltpu.make_async_copy(labr.at[pl.ds(0, 7)], labr.at[pl.ds(0, 7)], lab_rs).wait()
    spread_row = lax.broadcasted_iota(jnp.int32, (64, 256), 0)
    spread_col = lax.broadcasted_iota(jnp.int32, (64, 256), 1)
    spread = (spread_row // 8 == spread_col // 32) & (spread_row % 8 == (spread_col // 16) % 2)
    by_device = tdot(labr[...].reshape(64, 128).astype(BF), spread.astype(F32).astype(BF)).astype(BF)
    chunk = lax.broadcasted_iota(jnp.int32, (16, 128), 0)
    far = 4 - (chunk + 1) // 2
    chunk_z = (z + jnp.where(chunk % 2 == 1, far, -far) + 16) % 8
    pick = lax.broadcasted_iota(jnp.int32, (16, 128), 1) == (x * 8 + chunk_z) * 2 + c
    labels = dot(pick.astype(F32).astype(BF), by_device)
    column = lax.broadcasted_iota(jnp.int32, (16, 256), 1)
    vrow[...] = labels * 16.0 + (column % 16).astype(F32)
    tall_row = lax.broadcasted_iota(jnp.int32, (256, 256), 0).astype(F32)
    for i in range(8):
        hots[i] = jnp.where(tall_row == vrow[i:i + 1, :], 1.0, 0.0).astype(BF)

    first = (b * 64 + me) * LEAF_DEV - HALO

    def near_step(s, carry):
        tall = jnp.concatenate([nb[s, :, 128 * j:128 * (j + 1)] for j in range(NEAR // 2)], axis=0)
        even = jnp.concatenate([pad[(ns[s, 2 * j] - first) & 31] for j in range(NEAR // 2)], axis=0)
        odd = jnp.concatenate([pad[(ns[s, 2 * j + 1] - first) & 31] for j in range(NEAR // 2)], axis=0)
        both = tdot(tall, jnp.concatenate([even, odd], axis=1))
        near[s] = both[:LEAF, :NRHS] + both[LEAF:, NRHS:]
        return carry

    def parents():
        loads[4].wait()
        loads[9].wait()
        for k in range(1, 4):
            pc_copy(k).wait_recv()
        picked = jnp.concatenate([pcr[jnp.clip(us[0, k] - 1, 0, 2)] for k in range(KU)], axis=1)
        both = tdot(uv[0], picked)
        parent_down = (both[:RANK, :NRHS] + both[RANK:, NRHS:]).astype(BF)
        lifted = jnp.concatenate([jnp.zeros((RANK, NRHS), BF), parent_down], axis=0)
        down_from_parent[...] = dot(tv[...].reshape(LEAF_DEV * RANK, 2 * RANK), lifted).reshape(
            LEAF_DEV, 4, 16, NRHS
        )


    def slots(i, h):
        region = xr.at[i, pl.ds(2 * h, 2), pl.ds(0, 7)]
        pltpu.make_async_copy(region, region, xr_sem.at[i, h]).wait()
        blocks = jnp.concatenate([xr[i, 2 * h + q].reshape(256, NRHS) for q in range(2)], axis=1)
        sums = dot(hots[i], blocks)
        return [sums[:, q * NRHS:(q + 1) * NRHS] for q in range(2)]

    def z_copy(i, h, sign):
        rows = pl.ds(0, 256) if i else pl.ds(0 if sign > 0 else 128, 128)
        place = 7 if i == 0 and sign < 0 else i
        return pltpu.make_async_remote_copy(
            zs.at[i, h, :, rows],
            zr.at[i, h, :, rows],
            zs_sem.at[place, h],
            zr_sem.at[place, h],
            device_id=up if sign > 0 else low,
            device_id_type=MESH,
        )

    def unit(i, h):
        sums = slots(i, h)
        if i == 0:
            for q in range(2):
                zs[i, h, q] = sums[q].astype(BF)
            z_copy(i, h, 1).start()
            z_copy(i, h, -1).start()
            return
        if i == 7:
            z_copy(5, h, 1).wait_recv()
            z_copy(6, h, -1).wait_recv()
            for q in range(2):
                total = sums[q] + zr[5, h, q].astype(F32) + zr[6, h, q].astype(F32)
                total = total.reshape(LEAF_DEV, 16, NRHS) + down_from_parent[:, 2 * h + q]
                downs[:, 2 * h + q] = total.astype(BF)
            return
        sign = 1 if i % 2 else -1
        before = max(i - 2, 0)
        z_copy(before, h, sign).wait_recv()
        for q in range(2):
            if before:
                zs[i, h, q] = (sums[q] + zr[before, h, q].astype(F32)).astype(BF)
            else:
                met = slice(0, 128) if sign > 0 else slice(128, 256)
                rest = slice(128, 256) if sign > 0 else slice(0, 128)
                zs[i, h, q, met] = (sums[q][met] + zr[0, h, q, met].astype(F32)).astype(BF)
                zs[i, h, q, rest] = sums[q][rest].astype(BF)
        z_copy(i, h, sign).start()

    unit(0, 0)
    unit(0, 1)
    issue(rounds[2])
    for n in range(2):
        halo_copy(n).wait_recv()
    loads[5].wait()
    loads[8].wait()
    done = 0
    for n, chunks in enumerate(rounds[1:4]):
        if n < 2:
            issue(rounds[n + 3])
        for h in range(2):
            for i in chunks:
                unit(i, h)
                if done == 0:
                    parents()
                if done < 8:
                    lax.fori_loop(2 * done, 2 * done + 2, near_step, 0, unroll=True)
                done += 1

    sent = xs.at[pl.ds(0, 7)]
    unit(7, 0)
    unit(7, 1)

    nothing = jnp.zeros((RANK, NRHS), BF)

    def out_step(s, carry):
        pair = [jnp.concatenate([nothing, downs[2 * s + n].reshape(RANK, NRHS)], axis=0) for n in range(2)]
        both = dot(bv[pl.ds(2 * s, 2)].reshape(2 * LEAF, 2 * RANK), jnp.concatenate(pair, axis=1))
        out[2 * s] = (both[:LEAF, :NRHS] + near[2 * s]).astype(BF)
        out[2 * s + 1] = (both[LEAF:, NRHS:] + near[2 * s + 1]).astype(BF)
        return carry

    lax.fori_loop(0, LEAF_DEV // 2, out_step, 0, unroll=True)

    pltpu.make_async_copy(sent, sent, xs_sem).wait()
    for n in range(2):
        halo_copy(n).wait_send()
    pltpu.make_async_copy(labr.at[pl.ds(0, 7)], labr.at[pl.ds(0, 7)], lab_ss).wait()
    for k in range(1, 4):
        pc_copy(k).wait_send()
    for h in range(2):
        z_copy(0, h, -1).wait_send()
        for i in range(7):
            z_copy(i, h, 1 if i == 0 or i % 2 else -1).wait_send()


def per_device(
    charges, near_src, near_block, bases, transfers, couple, far_dev, far_leaf, upper_couple, upper_src
):
    hbm = pl.BlockSpec(memory_space=pltpu.HBM)
    dma = pltpu.SemaphoreType.DMA
    out = pl.pallas_call(
        kernel,
        name="adjoint",
        out_shape=pltpu.VMEM((LEAF_DEV, LEAF, NRHS), BF),
        in_specs=[hbm] * 10,
        out_specs=pl.BlockSpec(memory_space=pltpu.VMEM),
        scratch_shapes=[
            pltpu.SMEM((FAR, LEAF_DEV), jnp.int32),
            pltpu.SMEM((FAR, LEAF_DEV), jnp.int32),
            pltpu.SMEM((LEAF_DEV, NEAR), jnp.int32),
            pltpu.SMEM((1, KU), jnp.int32),
            pltpu.VMEM((LEAF_DEV + 2 * HALO, LEAF, NRHS), BF),
            pltpu.VMEM((LEAF_DEV, LEAF, NEAR * LEAF), BF),
            pltpu.VMEM((LEAF_DEV, LEAF, 2 * RANK), BF),
            pltpu.VMEM((LEAF_DEV, RANK, 2 * RANK), BF),
            pltpu.VMEM((LEAF_DEV, RANK, FAR * RANK), BF),
            pltpu.VMEM((1, RANK, KU * RANK), BF),
            pltpu.VMEM((LEAF_DEV, RANK, NRHS), BF),
            pltpu.VMEM((PAIRS + 1, 4, 16, NRHS), BF),
            pltpu.VMEM((8, 128), jnp.int32),
            pltpu.SMEM((8, 128), jnp.int32),
            pltpu.VMEM((8, 128), F32),
            pltpu.VMEM((8, 8, 128), F32),
            pltpu.VMEM((8, 8, 4, 32, NRHS), BF),
            pltpu.VMEM((8, 4, 8, 32, NRHS), BF),
            pltpu.VMEM((16, 256), F32),
            pltpu.VMEM((8, 256, 256), BF),
            pltpu.VMEM((7, 2, 2, 256, NRHS), BF),
            pltpu.VMEM((7, 2, 2, 256, NRHS), BF),
            pltpu.VMEM((RANK, NRHS), BF),
            pltpu.VMEM((3, RANK, NRHS), BF),
            pltpu.VMEM((LEAF_DEV, 4, 16, NRHS), F32),
            pltpu.VMEM((LEAF_DEV, LEAF, NRHS), F32),
            pltpu.VMEM((LEAF_DEV, 4, 16, NRHS), BF),
            dma((10,)),
            dma,
            dma((2,)),
            dma((2,)),
            dma,
            dma,
            dma((3,)),
            dma((3,)),
            dma,
            dma((8, 2)),
            dma((8, 2)),
            dma((8, 2)),
            pltpu.SemaphoreType.REGULAR,
        ],
        compiler_params=pltpu.CompilerParams(
            collective_id=0, has_side_effects=True, vmem_limit_bytes=24 * 1024 * 1024
        ),
    )(
        *[
            pltpu.with_memory_space_constraint(a, pltpu.HBM)
            for a in (
                far_dev.T, far_leaf.T, near_src, upper_src,
                charges.reshape(LEAF_DEV, LEAF, NRHS), near_block, bases, transfers, couple, upper_couple,
            )
        ]
    )
    return out.reshape(LEAF_DEV * LEAF, NRHS)


def solution(mesh):
    rows = P(("branch", "leaf"), None)
    blocks = P(("branch", "leaf"), None, None)
    in_specs = (rows, rows, blocks, blocks, blocks, blocks, rows, rows, blocks, rows)
    return jax.shard_map(per_device, mesh=mesh, in_specs=in_specs, out_specs=rows, check_vma=False)
```
